128 devices in a mesh: dom: 8 (over y, core), slab: 16 (over z, x).
Axes of the slice: x: 4, y: 4, z: 4, core: 2. Of those that a mesh axis runs over, the one named last changes fastest.
Arguments:
- heat_level: float32 [2097152], P(('dom', 'slab')), may hold values from -6 to 6
- emitting_vertex_position: int32 [128, 3, 3, 8192], P(('dom', 'slab')), may hold values from 0 to 16383
- corner_holder_shift: int32 [4, 64, 128, 512], P(None, 'dom', 'slab'), may hold values from 0 to 8, as said below
- corner_fetched_bucket: int32 [4, 64, 128, 512], P(None, 'dom', 'slab'), may hold values from 0 to 8191
- corner_factors: float32 [4, 64, 128, 512], P(None, 'dom', 'slab'), may hold values from 0.05 to 0.5
- diagonal_rigidity: float32 [64, 128, 512], P('dom', 'slab'), may hold values from 0.25 to 2
- boundary_vertex_position: int32 [128, 3, 3, 128], P(('dom', 'slab')), may hold values from 0 to 32767
- boundary_bucket_tally: int32 [128, 9], P(('dom', 'slab')), may hold values from 1 to 128, 576 in all within a row
- boundary_accepting_vertex: int32 [128, 3, 3, 128], P(('dom', 'slab')), may hold values from 0 to 16383
Outputs:
- displacement: float32 [3, 64, 128, 512], P(None, 'dom', 'slab')
- thermal_disp: float32 [3, 2097152], P(None, ('dom', 'slab'))
The draws below stay inside these ranges and needn't reach their ends.
Inputs may be any that keep to these rules, and one draw needn't show every extreme that they name: emitting_vertex_position stays below 16384. corner_holder_shift is 3 a + b for an offset (a, b) of the hex node's device that names a device inside the mesh.
All inputs are finite; a program needn't handle non-finite values.
Results may differ from the reference program's by a relative error of at most 0.0001.
Values sent between devices are 32-bit elements; how exact they have to be, the bound alone decides.
A program may use at most 192 MiB of HBM per device.

```python
import math
import jax
import jax.numpy as jnp
import numpy as np

CX = 8
CY = 8
CZ = 512
HEAT_POINTS_SHARE = 16384
SLOT = 8192
WSLOT = 128
ITERS = 4
NX = 64
NY = 128
NZ = 512
HEAT_MESH_POINTS = 2097152
N_DOM = 8
N_SLAB = 16
DEVICES = 128


def draw_corner_holder_shift(key, part):
    dom_total = NX // CX
    slab_total = NY // CY
    coarse_key = jax.random.fold_in(key, 11)
    other_key = jax.random.fold_in(key, 23)
    keep_key = jax.random.fold_in(key, 37)
    coarse = jax.random.randint(coarse_key, (NX, NY, NZ // 8), 0, 9)
    primary = jnp.repeat(coarse, 8, axis=2)
    other = jax.random.randint(other_key, (4, NX, NY, NZ), 0, 9)
    keep = jax.random.randint(keep_key, (4, NX, NY, NZ), 0, 4) < 3
    pick = jnp.where(keep, primary[None], other)
    offset_a = pick // 3
    offset_b = pick % 3
    dom_pos = (jnp.arange(NX, dtype=jnp.int32) // CX)[None, :, None, None]
    slab_pos = (jnp.arange(NY, dtype=jnp.int32) // CY)[None, None, :, None]
    near_dom = dom_pos + offset_a - 1
    near_slab = slab_pos + offset_b - 1
    inside = (near_dom >= 0) & (near_dom < dom_total) & (near_slab >= 0) & (near_slab < slab_total)
    return jnp.where(inside, pick, 4).astype(jnp.int32)


def place_ends(values, stream_key, least, top_value):
    longest = values.shape.index(max(values.shape))
    spots = []
    for shift in (0, 1):
        where = [jax.random.randint(jax.random.fold_in(stream_key, axis), (), 0, length) for axis, length in enumerate(values.shape)]
        where[longest] = (where[longest] + shift) % values.shape[longest]
        spots.append(tuple(where))
    return values.at[spots[0]].set(least).at[spots[1]].set(top_value)


def block_scale(stream_key, shape, split, smallest, top_value):
    factor_of = 1.0
    for position, blocks in split:
        draws = jax.random.uniform(jax.random.fold_in(jax.random.fold_in(stream_key, 6), position), (blocks,), jnp.float32, smallest / len(split), top_value / len(split))
        factor_of = factor_of * jnp.repeat(jnp.exp(draws), shape[position] // blocks).reshape((-1,) + (1,) * (len(shape) - 1 - position))
    return factor_of


def length_profile(amount, total, reach, lean):
    portions = [(1 << 20) // math.isqrt(grade ** lean) + 1 for grade in range(2, amount + 1)]
    spare, holding = total - reach - (amount - 1), [1] * (amount - 1)
    while spare > 0:
        movable = [i for i in range(amount - 1) if holding[i] < reach]
        whole, left = sum([portions[i] for i in movable]), spare
        for i in movable:
            more = min(reach - holding[i], max(1, left * portions[i] // whole), spare)
            holding[i] = holding[i] + more
            spare = spare - more
    return np.array([reach] + holding)


def ragged(own_key, count, total, bound, slope):
    if count == 2:
        one = jax.random.randint(own_key, (), max(1, total - bound), min(bound, total - 1) + 1)
        return jnp.stack([one, total - one])
    tallies = jnp.asarray(length_profile(count, total, bound, slope), jnp.int32)
    couples = (count - 1) // 2
    giver, taker = tallies[1:1 + 2 * couples:2], tallies[2:2 + 2 * couples:2]
    room = jnp.minimum(giver - 1, bound - taker)
    moved = jax.random.randint(jax.random.fold_in(own_key, 1), (couples,), 0, 1 << 20) % (room + 1)
    tallies = tallies.at[1:1 + 2 * couples:2].set(giver - moved).at[2:2 + 2 * couples:2].set(taker + moved)
    return tallies[jax.random.permutation(jax.random.fold_in(own_key, 2), count)]


def noise(key, dims, spread, limit, cuts=(), kind=jnp.bfloat16):
    level = block_scale(key, dims, cuts, -0.22, 0.18) if cuts else 1.0
    array = jax.random.normal(key, dims, jnp.float32) * spread * level
    return jnp.minimum(jnp.maximum(array, -limit), limit).astype(kind)


def setup_inputs(seed: int = 0) -> dict:
    key_of = jax.random.split(jax.random.key(seed), 10)
    return {
        "heat_level": noise(key_of[0], (HEAT_MESH_POINTS,), 1.0, 6.0, ((0, 128),), jnp.float32),
        "emitting_vertex_position": place_ends(jax.random.randint(key_of[1], (DEVICES, 3, 3, SLOT), 0, min(HEAT_POINTS_SHARE, 65280)), jax.random.fold_in(key_of[1], 1), 0, (min(HEAT_POINTS_SHARE, 65280)) - 1).astype(jnp.int32),
        "corner_holder_shift": draw_corner_holder_shift(jax.random.fold_in(key_of[9], 71), 0),
        "corner_fetched_bucket": place_ends(jax.random.randint(key_of[3], (4, NX, NY, NZ), 0, SLOT), jax.random.fold_in(key_of[3], 1), 0, SLOT - 1).astype(jnp.int32),
        "corner_factors": jnp.clip(0.05 + 0.45 * jax.random.uniform(key_of[4], (4, NX, NY, NZ), jnp.float32) ** block_scale(key_of[4], (4, NX, NY, NZ), ((1, 8), (2, 16)), -0.2, 0.2), 0.05, 0.5),
        "diagonal_rigidity": jnp.clip(0.25 + 1.75 * jax.random.uniform(key_of[5], (NX, NY, NZ), jnp.float32) ** block_scale(key_of[5], (NX, NY, NZ), ((0, 8), (1, 16)), -0.2, 0.2), 0.25, 2.0),
        "boundary_vertex_position": place_ends(jax.random.randint(key_of[6], (DEVICES, 3, 3, WSLOT), 0, CX * CY * CZ), jax.random.fold_in(key_of[6], 1), 0, (CX * CY * CZ) - 1).astype(jnp.int32),
        "boundary_bucket_tally": jax.vmap(lambda own: ragged(own, 9, 9 * WSLOT // 2, WSLOT, 2))(jax.random.split(key_of[7], DEVICES)).reshape((DEVICES, 9)).astype(jnp.int32),
        "boundary_accepting_vertex": place_ends(jax.random.randint(key_of[8], (DEVICES, 3, 3, WSLOT), 0, HEAT_POINTS_SHARE), jax.random.fold_in(key_of[8], 1), 0, HEAT_POINTS_SHARE - 1).astype(jnp.int32),
    }


COEF = 0.5


def operate(bucket_entries, diagonal_rigidity):
    padded = jnp.pad(bucket_entries, ((0, 0), (1, 1), (1, 1), (1, 1)))
    beside = padded[:, 2:, 1:-1, 1:-1] + padded[:, :-2, 1:-1, 1:-1]
    beside = beside + padded[:, 1:-1, 2:, 1:-1] + padded[:, 1:-1, :-2, 1:-1]
    beside = beside + padded[:, 1:-1, 1:-1, 2:] + padded[:, 1:-1, 1:-1, :-2]
    return (6.0 + diagonal_rigidity)[None] * bucket_entries - beside


def neighbour(dom_of, slab_of, offset_a, offset_b):
    near_dom = dom_of + offset_a - 1
    near_slab = slab_of + offset_b - 1
    inside = (near_dom >= 0) & (near_dom < N_DOM) & (near_slab >= 0) & (near_slab < N_SLAB)
    providing_holder = jnp.clip(near_dom, 0, N_DOM - 1) * N_SLAB + jnp.clip(near_slab, 0, N_SLAB - 1)
    return inside, providing_holder.astype(jnp.int32)


def reference(heat_level, emitting_vertex_position, corner_holder_shift, corner_fetched_bucket, corner_factors, diagonal_rigidity, boundary_vertex_position, boundary_bucket_tally, boundary_accepting_vertex):
    devices = N_DOM * N_SLAB
    dev_ids = jnp.arange(devices, dtype=jnp.int32)
    dom_of = dev_ids // N_SLAB
    slab_of = dev_ids % N_SLAB
    pieces = []
    for offset_a in range(3):
        for offset_b in range(3):
            inside, providing_holder = neighbour(dom_of, slab_of, offset_a, offset_b)
            device_portion = emitting_vertex_position[providing_holder, 2 - offset_a, 2 - offset_b]
            bucket_entries = heat_level[providing_holder[:, None] * HEAT_POINTS_SHARE + device_portion]
            pieces.append(jnp.where(inside[:, None], bucket_entries, jnp.zeros_like(bucket_entries)))
    received = jnp.stack(pieces, 1).reshape(devices, 9 * SLOT)
    owner_rows = (jnp.arange(NX, dtype=jnp.int32) // CX) * N_SLAB
    owner_map = owner_rows[:, None] + (jnp.arange(NY, dtype=jnp.int32) // CY)[None, :]
    interp = jnp.zeros((NX, NY, NZ), jnp.float32)
    for corner in range(4):
        column = corner_holder_shift[corner] * SLOT + corner_fetched_bucket[corner]
        interp = interp + corner_factors[corner] * received[owner_map[:, :, None], column]
    padded = jnp.pad(interp, 1)
    thermal_load = COEF * jnp.stack([
        padded[2:, 1:-1, 1:-1] - padded[:-2, 1:-1, 1:-1],
        padded[1:-1, 2:, 1:-1] - padded[1:-1, :-2, 1:-1],
        padded[1:-1, 1:-1, 2:] - padded[1:-1, 1:-1, :-2]])
    solution = jnp.zeros_like(thermal_load)
    residual = thermal_load
    direction = thermal_load
    norm_now = jnp.sum(residual * residual)
    for iteration in range(ITERS):
        applied = operate(direction, diagonal_rigidity)
        step_size = norm_now / jnp.sum(direction * applied)
        solution = solution + step_size * direction
        residual = residual - step_size * applied
        norm_next = jnp.sum(residual * residual)
        direction = residual + (norm_next / norm_now) * direction
        norm_now = norm_next
    src_ids = dev_ids[:, None, None, None]
    rows_x = (src_ids // N_SLAB) * CX + boundary_vertex_position // (CY * CZ)
    rows_y = (src_ids % N_SLAB) * CY + (boundary_vertex_position // CZ) % CY
    rows_z = boundary_vertex_position % CZ
    surface = solution[:, rows_x, rows_y, rows_z]
    live = jnp.arange(WSLOT, dtype=jnp.int32)[None, None, None, :] < boundary_bucket_tally.reshape(devices, 3, 3)[:, :, :, None]
    surface = jnp.where(live[None], surface, jnp.zeros_like(surface))
    thermal_disp = jnp.zeros((3, HEAT_MESH_POINTS), jnp.float32)
    for offset_a in range(3):
        for offset_b in range(3):
            inside, providing_holder = neighbour(dom_of, slab_of, offset_a, offset_b)
            bucket_entries = surface[:, providing_holder, 2 - offset_a, 2 - offset_b, :]
            bucket_entries = jnp.where(inside[None, :, None], bucket_entries, jnp.zeros_like(bucket_entries))
            targets = dev_ids[:, None] * HEAT_POINTS_SHARE + boundary_accepting_vertex[:, offset_a, offset_b, :]
            thermal_disp = thermal_disp.at[:, targets.reshape(-1)].add(bucket_entries.reshape(3, -1))
    return solution, thermal_disp
```

```python
import functools

import jax
import jax.numpy as jnp
from jax import lax
from jax.experimental import pallas as pl
from jax.experimental.pallas import tpu as pltpu
from jax.sharding import PartitionSpec as P

DOM = "dom"
SLAB = "slab"
BOTH = ("dom", "slab")
ITERS = 4
COEF = 0.5
CENTRE = 7.125
SPREAD = 6.875
VMEM = 56 * 2**20


def with_halo(shard, sides, width):
    for axis, dim in sides:
        peers, length = (lax.axis_size(axis), shard.shape[dim])
        up = [(i, i + 1) for i in range(peers - 1)]
        down = [(j, i) for i, j in up]
        last = lax.slice_in_dim(shard, length - width, length, axis=dim)
        leading = lax.slice_in_dim(shard, 0, width, axis=dim)
        before = lax.ppermute(last, axis, up)
        after = lax.ppermute(leading, axis, down)
        shard = jnp.concatenate([before, shard, after], axis=dim)
    return shard


def two_pieces(table):
    high = table.astype(jnp.bfloat16)
    low = (table - high.astype(jnp.float32)).astype(jnp.bfloat16)
    return high, low


def look_up(pieces_ref, groups, across, group):
    width = across.shape[1]
    hot = lax.broadcasted_iota(jnp.int32, (256, width), 0) == across
    hot = jnp.where(hot, 1.0, 0.0).astype(jnp.bfloat16)
    picked = jnp.dot(pieces_ref[...], hot, preferred_element_type=jnp.float32)
    picked = picked[:groups] + picked[groups:]
    apart = group - lax.broadcasted_iota(jnp.int32, (8, width), 0)
    total = jnp.zeros((8, width), jnp.float32)
    for k in range(groups // 8):
        total = jnp.where(apart == 8 * k, picked[8 * k : 8 * k + 8], total)
    return total


def pair_of_rows(ref, row):
    return jnp.concatenate([ref[pl.ds(row, 1), :], ref[pl.ds(row + 1, 1), :]], axis=1)


def slots_kernel(heat_ref, position_ref, out_ref, pieces_ref):
    table = jnp.concatenate([heat_ref[:64], heat_ref[64:]], axis=1)
    pieces_ref[:64], pieces_ref[64:] = two_pieces(table)

    def step(i, carry):
        for pair in range(8):
            row = 16 * i + 2 * pair
            k = pair_of_rows(position_ref, row)
            across = (k >> 13) * 128 + (k & 127)
            found = look_up(pieces_ref, 64, across, (k >> 7) & 63)
            found = jnp.sum(found, axis=0, keepdims=True)
            out_ref[pl.ds(row, 1), :] = found[:, :128]
            out_ref[pl.ds(row + 1, 1), :] = found[:, 128:]
        return carry

    lax.fori_loop(0, position_ref.shape[0] // 16, step, 0)


def interp_kernel(slots_ref, shift_ref, bucket_ref, factor_ref, out_ref, pieces_ref):
    for h in range(9):
        table = jnp.concatenate(
            [slots_ref[64 * h : 64 * h + 32], slots_ref[64 * h + 32 : 64 * h + 64]], axis=1
        )
        pieces_ref[32 * h : 32 * h + 32], pieces_ref[288 + 32 * h : 320 + 32 * h] = two_pieces(table)

    def step(i, carry):
        for pair in range(4):
            row = 8 * i + 2 * pair
            total = jnp.zeros((8, 256), jnp.float32)
            for corner in range(4):
                k = pair_of_rows(bucket_ref.at[corner], row)
                holder = pair_of_rows(shift_ref.at[corner], row)
                across = ((k >> 12) & 1) * 128 + (k & 127)
                found = look_up(pieces_ref, 288, across, holder * 32 + ((k >> 7) & 31))
                total = total + found * pair_of_rows(factor_ref.at[corner], row)
            total = jnp.sum(total, axis=0, keepdims=True)
            out_ref[pl.ds(row, 1), :] = total[:, :128]
            out_ref[pl.ds(row + 1, 1), :] = total[:, 128:]
        return carry

    lax.fori_loop(0, out_ref.shape[0] // 8, step, 0)


def call(kernel, rows, scratch, *args):
    return pl.pallas_call(
        kernel,
        out_shape=jax.ShapeDtypeStruct((rows, 128), jnp.float32),
        scratch_shapes=scratch,
        compiler_params=pltpu.CompilerParams(vmem_limit_bytes=VMEM),
    )(*args)


def fetch_entries(source_table, positions):
    entry_count = source_table.shape[0]
    table_rows = source_table.reshape(entry_count // 128, 128)
    picked = table_rows[positions // 128]
    chosen = jnp.arange(128, dtype=jnp.int32) == (positions % 128)[..., None]
    return jnp.sum(jnp.where(chosen, picked, jnp.zeros_like(picked)), axis=-1)


def spread_entries(values, positions, entry_count):
    row_count = entry_count // 128
    row_hot = ((positions // 128)[:, None] == jnp.arange(row_count)[None, :]).astype(jnp.float32)
    lane_hot = ((positions % 128)[:, None] == jnp.arange(128)[None, :]).astype(jnp.float32)
    weighted = values[:, :, None] * lane_hot[None]
    summed = jnp.einsum("kh,ckl->chl", row_hot, weighted, precision=lax.Precision.HIGHEST)
    return summed.reshape(values.shape[0], entry_count)


def scaled_operate(field, rigidity):
    inner = field[:, 1:-1, 1:-1, :]
    along_z = jnp.pad(inner, ((0, 0), (0, 0), (0, 0), (1, 1)))
    beside = field[:, 2:, 1:-1, :] + field[:, :-2, 1:-1, :]
    beside = beside + field[:, 1:-1, 2:, :] + field[:, 1:-1, :-2, :]
    beside = beside + along_z[:, :, :, 2:] + along_z[:, :, :, :-2]
    return ((6.0 - CENTRE + rigidity)[None] * inner - beside) * (1.0 / SPREAD)


def coefficients(moments):
    m = list(moments[:7])
    m[2], m[3] = 2.0 * m[2] - m[0], 2.0 * m[3] - m[1]
    m[4], m[5], m[6] = 2.0 * m[4] - m[0], 2.0 * m[5] - m[1], 2.0 * m[6] - m[0]
    gram = [[0.5 * (m[i + j] + m[abs(i - j)]) for j in range(4)] for i in range(4)]
    h = [[None] * 4 for _ in range(4)]
    for i in range(4):
        h[i][0] = gram[i][1]
        h[i][1] = 0.5 * (gram[i][0] + gram[i][2])
        h[i][2] = 0.5 * (gram[i][1] + gram[i][3])
    for i in range(3):
        h[i][3] = h[3][i]
    h[3][3] = moments[7]
    image = [[CENTRE * gram[i][j] + SPREAD * h[i][j] for j in range(4)] for i in range(4)]

    def form(matrix, v):
        n = len(v)
        return sum(
            (matrix[i][j] if i == j else 2.0 * matrix[i][j]) * v[i] * v[j]
            for i in range(n)
            for j in range(i, n)
        )

    one = jnp.ones_like(m[0])
    zero = jnp.zeros_like(m[0])
    x, r, p = [], [one], [one]
    rr = form(gram, r)
    for step in range(ITERS):
        alpha = rr / form(image, p)
        x = [(x[i] if i < len(x) else zero) + alpha * p[i] for i in range(len(p))]
        if step + 1 == ITERS:
            break
        shifted = [zero] * (len(p) + 1)
        for i, v in enumerate(p):
            shifted[i] = shifted[i] + CENTRE * v
            if i == 0:
                shifted[1] = shifted[1] + SPREAD * v
            else:
                shifted[i - 1] = shifted[i - 1] + 0.5 * SPREAD * v
                shifted[i + 1] = shifted[i + 1] + 0.5 * SPREAD * v
        r = [(r[i] if i < len(r) else zero) - alpha * shifted[i] for i in range(len(shifted))]
        new = form(gram, r)
        beta = new / rr
        p = [r[i] + beta * (p[i] if i < len(p) else zero) for i in range(len(r))]
        rr = new
    return x


def on_device(heat, emitting, shift, bucket, factors, rigidity, wet_position, wet_tally, accepting):
    dom_pos, slab_pos = lax.axis_index(DOM), lax.axis_index(SLAB)
    doms, slabs = lax.axis_size(DOM), lax.axis_size(SLAB)
    slots = call(
        slots_kernel,
        576,
        [pltpu.VMEM((128, 256), jnp.bfloat16)],
        heat.reshape(128, 128),
        emitting.reshape(576, 128),
    ).reshape(3, 3, 8192)
    wide = with_halo(rigidity, ((DOM, 0), (SLAB, 1)), 3)
    gathered = with_halo(slots, ((DOM, 0), (SLAB, 1)), 1)
    received = gathered[::2, ::2, :].reshape(576, 128)
    interp = call(
        interp_kernel,
        256,
        [pltpu.VMEM((576, 256), jnp.bfloat16)],
        received,
        shift.reshape(4, 256, 128),
        bucket.reshape(4, 256, 128),
        factors.reshape(4, 256, 128),
    ).reshape(8, 8, 512)
    deep = with_halo(interp, ((DOM, 0), (SLAB, 1)), 5)
    along_z = jnp.pad(deep[1:-1, 1:-1], ((0, 0), (0, 0), (1, 1)))
    load = COEF * jnp.stack(
        [
            deep[2:, 1:-1] - deep[:-2, 1:-1],
            deep[1:-1, 2:] - deep[1:-1, :-2],
            along_z[:, :, 2:] - along_z[:, :, :-2],
        ]
    )
    x_at = dom_pos * 8 - 4 + jnp.arange(16, dtype=jnp.int32)
    y_at = slab_pos * 8 - 4 + jnp.arange(16, dtype=jnp.int32)
    inside = ((x_at >= 0) & (x_at < 8 * doms))[:, None] & ((y_at >= 0) & (y_at < 8 * slabs))[None]

    def keep(field, depth):
        cut = inside[4 - depth : 12 + depth, 4 - depth : 12 + depth]
        return jnp.where(cut[None, :, :, None], field, jnp.zeros_like(field))

    def near(depth):
        return wide[3 - depth : 11 + depth, 3 - depth : 11 + depth]

    w0 = keep(load, 4)
    w1 = keep(scaled_operate(w0, near(3)), 3)
    w2 = keep(2.0 * scaled_operate(w1, near(2)) - w0[:, 2:-2, 2:-2], 2)
    w3 = keep(2.0 * scaled_operate(w2, near(1)) - w1[:, 2:-2, 2:-2], 1)
    last = scaled_operate(w3, near(0))
    w0, w1, w2, w3 = w0[:, 4:-4, 4:-4], w1[:, 3:-3, 3:-3], w2[:, 2:-2, 2:-2], w3[:, 1:-1, 1:-1]
    pairs = ((w0, w0), (w0, w1), (w1, w1), (w1, w2), (w2, w2), (w2, w3), (w3, w3), (w3, last))
    moments = lax.psum(jnp.stack([jnp.sum(a * b) for a, b in pairs]), BOTH)
    c = coefficients([moments[i] for i in range(8)])
    solution = c[0] * w0 + c[1] * w1 + c[2] * w2 + c[3] * w3

    flat = solution.reshape(3, -1)
    surface = jnp.stack([fetch_entries(flat[a], wet_position[0]) for a in range(3)])
    live = jnp.arange(128, dtype=jnp.int32)[None, None, :] < wet_tally[0].reshape(3, 3)[:, :, None]
    surface = jnp.where(live[None], surface, jnp.zeros_like(surface))
    returned = with_halo(surface, ((DOM, 1), (SLAB, 2)), 1)
    arrived = returned[:, ::2, ::2, :]
    thermal_disp = spread_entries(arrived.reshape(3, -1), accepting[0].reshape(-1), heat.shape[0])
    return solution, thermal_disp


def solution(mesh):
    in_specs = (
        P(BOTH),
        P(BOTH, None, None, None),
        P(None, DOM, SLAB, None),
        P(None, DOM, SLAB, None),
        P(None, DOM, SLAB, None),
        P(DOM, SLAB, None),
        P(BOTH, None, None, None),
        P(BOTH, None),
        P(BOTH, None, None, None),
    )
    out_specs = (P(None, DOM, SLAB, None), P(None, BOTH))
    return jax.shard_map(on_device, mesh=mesh, in_specs=in_specs, out_specs=out_specs, check_vma=False)
```

```python
import functools

import jax
import jax.numpy as jnp
from jax import lax
from jax.experimental import pallas as pl
from jax.experimental.pallas import tpu as pltpu
from jax.sharding import PartitionSpec as P

DOM = "dom"
SLAB = "slab"
BOTH = ("dom", "slab")
MESH = pl.DeviceIdType.MESH
ITERS = 4
COEF = 0.5
CENTRE = 7.125
SPREAD = 6.875
F32 = jnp.float32
BF16 = jnp.bfloat16


def two_pieces(table):
    high = table.astype(BF16)
    low = (table - high.astype(F32)).astype(BF16)
    return high, low


def one_hot(across):
    width = across.shape[1]
    hot = lax.broadcasted_iota(jnp.int32, (256, width), 0) == across
    return jnp.where(hot, 1.0, 0.0).astype(BF16)


def pick_group(picked, groups, group):
    width = group.shape[1]
    picked = picked[:groups] + picked[groups:]
    apart = group - lax.broadcasted_iota(jnp.int32, (8, width), 0)
    total = jnp.zeros((8, width), F32)
    for k in range(groups // 8):
        total = jnp.where(apart == 8 * k, picked[8 * k : 8 * k + 8], total)
    return total


def look_up(pieces_ref, groups, across, group):
    picked = jnp.dot(pieces_ref[...], one_hot(across), preferred_element_type=F32)
    return pick_group(picked, groups, group)


def coefficients(moments):
    m = list(moments[:7])
    m[2], m[3] = 2.0 * m[2] - m[0], 2.0 * m[3] - m[1]
    m[4], m[5], m[6] = 2.0 * m[4] - m[0], 2.0 * m[5] - m[1], 2.0 * m[6] - m[0]
    gram = [[0.5 * (m[i + j] + m[abs(i - j)]) for j in range(4)] for i in range(4)]
    h = [[None] * 4 for _ in range(4)]
    for i in range(4):
        h[i][0] = gram[i][1]
        h[i][1] = 0.5 * (gram[i][0] + gram[i][2])
        h[i][2] = 0.5 * (gram[i][1] + gram[i][3])
    for i in range(3):
        h[i][3] = h[3][i]
    h[3][3] = moments[7]
    image = [[CENTRE * gram[i][j] + SPREAD * h[i][j] for j in range(4)] for i in range(4)]

    def form(matrix, v):
        n = len(v)
        return sum(
            (matrix[i][j] if i == j else 2.0 * matrix[i][j]) * v[i] * v[j]
            for i in range(n)
            for j in range(i, n)
        )

    one = jnp.ones_like(m[0])
    zero = jnp.zeros_like(m[0])
    x, r, p = [], [one], [one]
    rr = form(gram, r)
    for step in range(ITERS):
        alpha = rr / form(image, p)
        x = [(x[i] if i < len(x) else zero) + alpha * p[i] for i in range(len(p))]
        if step + 1 == ITERS:
            break
        shifted = [zero] * (len(p) + 1)
        for i, v in enumerate(p):
            shifted[i] = shifted[i] + CENTRE * v
            if i == 0:
                shifted[1] = shifted[1] + SPREAD * v
            else:
                shifted[i - 1] = shifted[i - 1] + 0.5 * SPREAD * v
                shifted[i + 1] = shifted[i + 1] + 0.5 * SPREAD * v
        r = [(r[i] if i < len(r) else zero) - alpha * shifted[i] for i in range(len(shifted))]
        new = form(gram, r)
        beta = new / rr
        p = [r[i] + beta * (p[i] if i < len(p) else zero) for i in range(len(r))]
        rr = new
    return x


def half_turn(tile):
    return pltpu.roll(tile, 4, 0)


def low_half(tile):
    return lax.broadcasted_iota(jnp.int32, tile.shape, 0) < 4


def pack_halos(block, side, corner, fifth):
    for x in range(4):
        near, far = block[x], block[x + 4]
        side[0, x] = jnp.where(low_half(near), near, half_turn(far))
        side[1, x] = jnp.where(low_half(near), half_turn(near), far)
    if fifth:
        for x in range(8):
            side[0, 4, x : x + 1] = block[x, 4:5]
            side[1, 4, x : x + 1] = block[x, 3:4]
    for a in range(2):
        for j in range(2):
            near, far = block[4 * a + j], block[4 * a + 2 + j]
            corner[a, 0, j] = jnp.where(low_half(near), near, half_turn(far))
            corner[a, 1, j] = jnp.where(low_half(near), half_turn(near), far)


def unpack_halos(block, side, dom, corner, wide):
    def put(at, middle, left, right):
        turned = half_turn(middle)
        wide[at, 0:8] = jnp.where(low_half(turned), left, turned)
        wide[at, 8:16] = jnp.where(low_half(turned), turned, right)

    for x in range(8):
        left, right = side[0, x % 4], side[1, x % 4]
        if x < 4:
            right = half_turn(right)
        else:
            left = half_turn(left)
        put(5 + x, block[x], left, right)
    for a in range(2):
        for t in range(5):
            u = t - 1 if a == 0 else t
            if 0 <= u < 4:
                left, right = corner[a, 0, u % 2], corner[a, 1, u % 2]
                if u < 2:
                    right = half_turn(right)
                else:
                    left = half_turn(left)
            else:
                left = right = jnp.zeros((8, 512), F32)
            put(t if a == 0 else 13 + t, dom[a, t], left, right)


def kernel(
    doms,
    slabs,
    heat,
    emitting,
    shift_hbm,
    bucket_hbm,
    factor_hbm,
    rigidity,
    wet_position,
    wet_tally,
    accepting,
    disp,
    spread,
    shift,
    bucket,
    factor,
    heat_pieces,
    slots_out,
    slots_in,
    pieces,
    interp,
    side_out,
    side_in,
    dom_in,
    corner_out,
    corner_in,
    rig_side_out,
    rig_side_in,
    rig_dom_in,
    rig_corner_out,
    rig_corner_in,
    wide,
    rig_wide,
    basis,
    centre,
    dom_moments,
    slab_moments,
    wet_pieces,
    wet_out,
    wet_in,
    load_sem,
    slot_send,
    slot_recv,
    halo_send,
    halo_recv,
    rig_send,
    rig_recv,
    wet_send,
    wet_recv,
    dom_send,
    dom_recv,
    slab_send,
    slab_recv,
):
    d, s = lax.axis_index(DOM), lax.axis_index(SLAB)

    def exists(a, b):
        return (d + a >= 1) & (d + a <= doms) & (s + b >= 1) & (s + b <= slabs)

    loads = [
        pltpu.make_async_copy(src, dst, load_sem.at[i])
        for i, (src, dst) in enumerate(((shift_hbm, shift), (bucket_hbm, bucket), (factor_hbm, factor)))
    ]
    for load in loads:
        load.start()

    barrier = pltpu.get_barrier_semaphore()
    for k in range(1, doms):
        pl.semaphore_signal(barrier, inc=1, device_id=(lax.rem(d + k, doms), s), device_id_type=MESH)
    for k in range(1, slabs):
        pl.semaphore_signal(barrier, inc=1, device_id=(d, lax.rem(s + k, slabs)), device_id_type=MESH)
    expected = doms + slabs - 2
    for a in (0, 2):
        for b in (0, 2):

            @pl.when(exists(a, b))
            def _():
                pl.semaphore_signal(
                    barrier, inc=1, device_id=(d + (a - 1), s + (b - 1)), device_id_type=MESH
                )

            expected = expected + exists(a, b).astype(jnp.int32)

    def halo_copies(block, s_out, s_in, d_in, c_out, c_in, send, recv):
        found = []
        for a in range(3):
            for b in range(3):
                if a == 1 and b == 1:
                    continue
                if a == 1:
                    src, dst = s_out.at[b // 2], s_in.at[1 - b // 2]
                elif b == 1:
                    src, dst = block.at[pl.ds(3 if a == 2 else 0, 5)], d_in.at[1 - a // 2]
                else:
                    src, dst = c_out.at[a // 2, b // 2], c_in.at[1 - a // 2, 1 - b // 2]
                j = 3 * a + b
                copy = pltpu.make_async_remote_copy(
                    src_ref=src,
                    dst_ref=dst,
                    send_sem=send.at[j],
                    recv_sem=recv.at[8 - j],
                    device_id=(d + (a - 1), s + (b - 1)),
                    device_id_type=MESH,
                )
                found.append((a, b, copy))
        return found

    def start_all(copies):
        for a, b, copy in copies:

            @pl.when(exists(a, b))
            def _():
                copy.start()

    def receive_all(copies):
        for a, b, copy in copies:

            @pl.when(exists(2 - a, 2 - b))
            def _():
                copy.wait_recv()

    def finish_all(copies):
        for a, b, copy in copies:

            @pl.when(exists(a, b))
            def _():
                copy.wait_send()

    def clear_missing(s_in, d_in, c_in):
        for a in range(3):
            for b in range(3):
                if a == 1 and b == 1:
                    continue

                @pl.when(jnp.logical_not(exists(a, b)))
                def _():
                    if a == 1:
                        s_in[b // 2] = jnp.zeros((5, 8, 512), F32)
                    elif b == 1:
                        d_in[a // 2] = jnp.zeros((5, 8, 512), F32)
                    else:
                        c_in[a // 2, b // 2] = jnp.zeros((2, 8, 512), F32)

    def clear_blocks(blocks):
        for j in range(9):
            if j == 4:
                continue

            @pl.when(jnp.logical_not(exists(j // 3, j % 3)))
            def _():
                blocks[j] = jnp.zeros(blocks.shape[1:], F32)

    heat_pieces[:64], heat_pieces[64:] = two_pieces(jnp.concatenate([heat[:64], heat[64:]], axis=1))
    pack_halos(rigidity, rig_side_out, rig_corner_out, False)
    for b in range(2):
        rig_side_out[b, 4] = jnp.zeros((8, 512), F32)
    clear_missing(rig_side_in, rig_dom_in, rig_corner_in)
    clear_missing(side_in, dom_in, corner_in)
    clear_blocks(slots_in)
    clear_blocks(wet_in)
    wet_out[...] = jnp.zeros(wet_out.shape, F32)
    pl.semaphore_wait(barrier, expected)
    rig_copies = halo_copies(
        rigidity, rig_side_out, rig_side_in, rig_dom_in, rig_corner_out, rig_corner_in, rig_send, rig_recv
    )
    start_all(rig_copies)

    def slot_copy(j):
        return pltpu.make_async_remote_copy(
            src_ref=slots_out.at[j],
            dst_ref=slots_in.at[8 - j],
            send_sem=slot_send.at[j],
            recv_sem=slot_recv.at[8 - j],
            device_id=(d + (j // 3 - 1), s + (j % 3 - 1)),
            device_id_type=MESH,
        )

    def slot_block(t, carry):
        j = lax.rem(t + 5, 9)
        a, b = j // 3, lax.rem(j, 3)

        def chunk(q, carry):
            for i in range(16):
                at = pl.multiple_of(4096 * q + 256 * i, 256)
                k = emitting[0, a, pl.ds(b, 1), pl.ds(at, 256)]
                across = (k >> 13) * 128 + (k & 127)
                found = look_up(heat_pieces, 64, across, (k >> 7) & 63)
                slots_out[j, pl.ds(16 * q + i, 1), :] = jnp.sum(found, axis=0, keepdims=True)
            return carry

        lax.fori_loop(0, 2, chunk, 0)

        @pl.when((j != 4) & exists(a, b))
        def _():
            slot_copy(j).start()

        return carry

    lax.fori_loop(0, 9, slot_block, 0)
    slots_in[4] = slots_out[4]
    for load in loads:
        load.wait()
    for j in range(9):
        if j == 4:
            continue

        @pl.when(exists(2 - j // 3, 2 - j % 3))
        def _():
            slot_copy(j).wait_recv()

    for h in range(9):
        pieces[32 * h : 32 * h + 32], pieces[288 + 32 * h : 320 + 32 * h] = two_pieces(slots_in[h])

    def plane(x, carry):
        def rows(q, carry):
            for i in range(2):
                for half in range(2):
                    y = 2 * q + i
                    total = jnp.zeros((8, 256), F32)
                    for corner in range(4):
                        at = (corner, x, pl.ds(y, 1), pl.ds(256 * half, 256))
                        k = bucket[at]
                        found = look_up(pieces, 288, k & 255, shift[at] * 32 + (k >> 8))
                        total = total + found * factor[at]
                    interp[x, pl.ds(y, 1), pl.ds(256 * half, 256)] = jnp.sum(total, axis=0, keepdims=True)
            return carry

        return lax.fori_loop(0, 4, rows, carry)

    lax.fori_loop(0, 8, plane, 0)

    pack_halos(interp, side_out, corner_out, True)
    copies = halo_copies(interp, side_out, side_in, dom_in, corner_out, corner_in, halo_send, halo_recv)
    start_all(copies)
    receive_all(rig_copies)
    unpack_halos(rigidity, rig_side_in, rig_dom_in, rig_corner_in, rig_wide)
    receive_all(copies)
    unpack_halos(interp, side_in, dom_in, corner_in, wide)

    row = lax.broadcasted_iota(jnp.int32, (16, 512), 0)
    lane = lax.broadcasted_iota(jnp.int32, (16, 512), 1)
    row_inside = ((row >= 4) | (s > 0)) & ((row < 12) | (s < slabs - 1))

    def inside(xx):
        return row_inside & ((xx >= 4) | (d > 0)) & ((xx < 12) | (d < doms - 1))

    def back_z(v):
        return jnp.where(lane == 0, 0.0, pltpu.roll(v, 1, 1))

    def ahead_z(v):
        return jnp.where(lane == 511, 0.0, pltpu.roll(v, 511, 1))

    def load_plane(xx, carry):
        here = wide[xx + 1]
        keep = inside(xx)
        at = jnp.clip(xx - 4, 0, 7)
        back = jnp.where(row == 0, side_in[0, 4, pl.ds(at, 1), :], pltpu.roll(here, 1, 0))
        ahead = jnp.where(row == 15, side_in[1, 4, pl.ds(at, 1), :], pltpu.roll(here, 15, 0))
        basis[0, 0, xx] = jnp.where(keep, COEF * (wide[xx + 2] - wide[xx]), 0.0)
        basis[0, 1, xx] = jnp.where(keep, COEF * (ahead - back), 0.0)
        basis[0, 2, xx] = jnp.where(keep, COEF * (ahead_z(here) - back_z(here)), 0.0)
        return carry

    lax.fori_loop(0, 16, load_plane, 0)

    def scaled_operate(level, c, xx):
        v = basis[level, c, xx]
        beside = basis[level, c, xx - 1] + basis[level, c, xx + 1]
        beside = beside + pltpu.roll(v, 1, 0) + pltpu.roll(v, 15, 0)
        beside = beside + back_z(v) + ahead_z(v)
        return ((rig_wide[xx + 1] + (6.0 - CENTRE)) * v - beside) * (1.0 / SPREAD)

    for level in range(1, 4):

        def next_plane(xx, carry, level=level):
            keep = inside(xx)
            for c in range(3):
                image = scaled_operate(level - 1, c, xx)
                if level > 1:
                    image = 2.0 * image - basis[level - 2, c, xx]
                basis[level, c, xx] = jnp.where(keep, image, 0.0)
            return carry

        lax.fori_loop(level, 16 - level, next_plane, 0)

    def folded(field):
        return jnp.where(low_half(field[:8]), field[8:], field[:8])

    def moment_plane(xx, totals):
        totals = list(totals)
        for c in range(3):
            w = [folded(basis[level, c, xx]) for level in range(4)]
            for level in range(4):
                centre[level, c, xx - 4] = w[level]
            w.append(folded(scaled_operate(3, c, xx)))
            pairs = ((0, 0), (0, 1), (1, 1), (1, 2), (2, 2), (2, 3), (3, 3), (3, 4))
            for i, (one, two) in enumerate(pairs):
                product = w[one] * w[two]
                product = (product[:, :128] + product[:, 128:256]) + (product[:, 256:384] + product[:, 384:])
                totals[i] = totals[i] + product
        return tuple(totals)

    totals = lax.fori_loop(4, 12, moment_plane, tuple(jnp.zeros((8, 128), F32) for _ in range(8)))
    for i in range(8):
        dom_moments[0, i : i + 1] = jnp.sum(totals[i], axis=0, keepdims=True)

    def reduce_copies(buffer, send, recv, count, device_of):
        return [
            pltpu.make_async_remote_copy(
                src_ref=buffer.at[0],
                dst_ref=buffer.at[k],
                send_sem=send.at[k],
                recv_sem=recv.at[k],
                device_id=device_of(k),
                device_id_type=MESH,
            )
            for k in range(1, count)
        ]

    dom_copies = reduce_copies(dom_moments, dom_send, dom_recv, doms, lambda k: (lax.rem(d + k, doms), s))
    slab_copies = reduce_copies(slab_moments, slab_send, slab_recv, slabs, lambda k: (d, lax.rem(s + k, slabs)))
    for copy in dom_copies:
        copy.start()

    for level in range(4):
        for c in range(3):
            for x in range(8):
                for half in range(2):
                    high, low = two_pieces(centre[level, c, x, :, 256 * half : 256 * half + 256])
                    at = 16 * x + 8 * half
                    wet_pieces[3 * level + c, at : at + 8] = high
                    wet_pieces[3 * level + c, 128 + at : 136 + at] = low

    for copy in dom_copies:
        copy.wait_recv()
    total = dom_moments[0]
    for k in range(1, doms):
        total = total + dom_moments[k]
    slab_moments[0] = total
    for copy in slab_copies:
        copy.start()

    for a in range(3):
        node = jnp.concatenate([wet_position[0, a, b : b + 1, :] for b in range(3)], axis=1)
        hot = one_hot(node & 255)
        group = (node >> 12) * 16 + ((node >> 8) & 1) * 8 + (((node >> 9) + 4) & 7)
        slot = lax.broadcasted_iota(jnp.int32, (1, 128), 1)
        live = jnp.concatenate(
            [slot < wet_tally[0:1, 3 * a + b : 3 * a + b + 1] for b in range(3)], axis=1
        )

        def gather_field(kc, carry, a=a, hot=hot, group=group, live=live):
            picked = jnp.dot(wet_pieces[kc], hot, preferred_element_type=F32)
            found = jnp.sum(pick_group(picked, 128, group), axis=0, keepdims=True)
            found = jnp.where(live, found, 0.0)
            for b in range(3):
                wet_out[3 * a + b, pl.ds(kc, 1), :] = found[:, 128 * b : 128 * b + 128]
            return carry

        lax.fori_loop(0, 12, gather_field, 0)

    wet_copies = []
    for j in range(9):
        if j == 4:
            continue
        copy = pltpu.make_async_remote_copy(
            src_ref=wet_out.at[j],
            dst_ref=wet_in.at[8 - j],
            send_sem=wet_send.at[j],
            recv_sem=wet_recv.at[8 - j],
            device_id=(d + (j // 3 - 1), s + (j % 3 - 1)),
            device_id_type=MESH,
        )
        wet_copies.append((j // 3, j % 3, copy))
    start_all(wet_copies)
    wet_in[4] = wet_out[4]

    taker = jnp.concatenate(
        [accepting[0, a, b : b + 1, :] for a in range(3) for b in range(3)], axis=1
    )
    node_row = lax.broadcasted_iota(jnp.int32, (128, 1152), 0)
    row_hot = jnp.where(node_row == (taker >> 7), 1.0, 0.0).astype(BF16)

    for copy in slab_copies:
        copy.wait_recv()
    total = slab_moments[0]
    for k in range(1, slabs):
        total = total + slab_moments[k]
    c = coefficients([jnp.sum(total[i : i + 1], axis=1, keepdims=True) for i in range(8)])

    def combine(x, carry):
        for a in range(3):
            field = c[0] * centre[0, a, x]
            for level in range(1, 4):
                field = field + c[level] * centre[level, a, x]
            disp[a, x] = half_turn(field)
        return carry

    lax.fori_loop(0, 8, combine, 0)

    receive_all(wet_copies)
    lane_of = taker & 127
    for a in range(3):
        value = jnp.concatenate(
            [
                sum(c[level] * wet_in[j, 3 * level + a : 3 * level + a + 1, :] for level in range(4))
                for j in range(9)
            ],
            axis=1,
        )
        high = value.astype(BF16).astype(F32)
        parts = [
            jnp.where(node_row == lane_of, part, 0.0).astype(BF16) for part in (high, value - high)
        ]
        spread[a] = sum(
            lax.dot_general(row_hot, part, (((1,), (1,)), ((), ())), preferred_element_type=F32)
            for part in parts
        )

    finish_all(rig_copies)
    for j in range(9):
        if j == 4:
            continue

        @pl.when(exists(j // 3, j % 3))
        def _():
            slot_copy(j).wait_send()

    finish_all(copies)
    finish_all(wet_copies)
    for copy in dom_copies + slab_copies:
        copy.wait_send()


def on_device(doms, slabs, heat, *args):
    dma = pltpu.SemaphoreType.DMA
    vm = pltpu.VMEM
    halos_out = [vm((2, 5, 8, 512), F32), vm((2, 2, 2, 8, 512), F32)]
    halos_in = [vm((2, 5, 8, 512), F32), vm((2, 5, 8, 512), F32), vm((2, 2, 2, 8, 512), F32)]
    halos = [halos_out[0], halos_in[0], halos_in[1], halos_out[1], halos_in[2]]
    whole = pl.BlockSpec(memory_space=pltpu.VMEM)
    away = pl.BlockSpec(memory_space=pl.ANY)
    disp, spread = pl.pallas_call(
        functools.partial(kernel, doms, slabs),
        out_shape=[
            jax.ShapeDtypeStruct((3, 8, 8, 512), F32),
            jax.ShapeDtypeStruct((3, 128, 128), F32),
        ],
        in_specs=[whole, whole, away, away, away, whole, whole, whole, whole],
        out_specs=[whole, whole],
        scratch_shapes=[
            vm((4, 8, 8, 512), jnp.int32),
            vm((4, 8, 8, 512), jnp.int32),
            vm((4, 8, 8, 512), F32),
            vm((128, 256), BF16),
            vm((9, 32, 256), F32),
            vm((9, 32, 256), F32),
            vm((576, 256), BF16),
            vm((8, 8, 512), F32),
            *halos,
            *halos,
            vm((18, 16, 512), F32),
            vm((18, 16, 512), F32),
            vm((4, 3, 16, 16, 512), F32),
            vm((4, 3, 8, 8, 512), F32),
            vm((doms, 8, 128), F32),
            vm((slabs, 8, 128), F32),
            vm((12, 256, 256), BF16),
            vm((9, 16, 128), F32),
            vm((9, 16, 128), F32),
            dma((3,)),
            dma((9,)),
            dma((9,)),
            dma((9,)),
            dma((9,)),
            dma((9,)),
            dma((9,)),
            dma((9,)),
            dma((9,)),
            dma((doms,)),
            dma((doms,)),
            dma((slabs,)),
            dma((slabs,)),
        ],
        compiler_params=pltpu.CompilerParams(
            collective_id=0, has_side_effects=True, vmem_limit_bytes=56 * 2**20
        ),
    )(heat.reshape(128, 128), *args)
    return disp, spread.reshape(3, -1)


def solution(mesh):
    in_specs = (
        P(BOTH),
        P(BOTH, None, None, None),
        P(None, DOM, SLAB, None),
        P(None, DOM, SLAB, None),
        P(None, DOM, SLAB, None),
        P(DOM, SLAB, None),
        P(BOTH, None, None, None),
        P(BOTH, None),
        P(BOTH, None, None, None),
    )
    out_specs = (P(None, DOM, SLAB, None), P(None, BOTH))
    return jax.shard_map(
        functools.partial(on_device, mesh.shape[DOM], mesh.shape[SLAB]),
        mesh=mesh,
        in_specs=in_specs,
        out_specs=out_specs,
        check_vma=False,
    )
```

```python
import functools

import jax
import jax.numpy as jnp
from jax import lax
from jax.experimental import pallas as pl
from jax.experimental.pallas import tpu as pltpu
from jax.sharding import PartitionSpec as P

DOM = "dom"
SLAB = "slab"
BOTH = ("dom", "slab")
MESH = pl.DeviceIdType.MESH
ITERS = 4
COEF = 0.5
CENTRE = 7.125
SPREAD = 6.875
F32 = jnp.float32
BF16 = jnp.bfloat16


def two_pieces(table):
    high = table.astype(BF16)
    low = (table - high.astype(F32)).astype(BF16)
    return high, low


def one_hot(across):
    width = across.shape[1]
    hot = lax.broadcasted_iota(jnp.int32, (256, width), 0) == across
    return jnp.where(hot, 1.0, 0.0).astype(BF16)


def pick_group(picked, groups, group):
    width = group.shape[1]
    picked = picked[:groups] + picked[groups:]
    apart = group - lax.broadcasted_iota(jnp.int32, (8, width), 0)
    total = jnp.zeros((8, width), F32)
    for k in range(groups // 8):
        total = jnp.where(apart == 8 * k, picked[8 * k : 8 * k + 8], total)
    return total


def look_up(pieces_ref, groups, across, group):
    picked = jnp.dot(pieces_ref[...], one_hot(across), preferred_element_type=F32)
    return pick_group(picked, groups, group)


def coefficients(moments):
    m = list(moments[:7])
    m[2], m[3] = 2.0 * m[2] - m[0], 2.0 * m[3] - m[1]
    m[4], m[5], m[6] = 2.0 * m[4] - m[0], 2.0 * m[5] - m[1], 2.0 * m[6] - m[0]
    gram = [[0.5 * (m[i + j] + m[abs(i - j)]) for j in range(4)] for i in range(4)]
    h = [[None] * 4 for _ in range(4)]
    for i in range(4):
        h[i][0] = gram[i][1]
        h[i][1] = 0.5 * (gram[i][0] + gram[i][2])
        h[i][2] = 0.5 * (gram[i][1] + gram[i][3])
    for i in range(3):
        h[i][3] = h[3][i]
    h[3][3] = moments[7]
    image = [[CENTRE * gram[i][j] + SPREAD * h[i][j] for j in range(4)] for i in range(4)]

    def form(matrix, v):
        n = len(v)
        return sum(
            (matrix[i][j] if i == j else 2.0 * matrix[i][j]) * v[i] * v[j]
            for i in range(n)
            for j in range(i, n)
        )

    one = jnp.ones_like(m[0])
    zero = jnp.zeros_like(m[0])
    x, r, p = [], [one], [one]
    rr = form(gram, r)
    for step in range(ITERS):
        alpha = rr / form(image, p)
        x = [(x[i] if i < len(x) else zero) + alpha * p[i] for i in range(len(p))]
        if step + 1 == ITERS:
            break
        shifted = [zero] * (len(p) + 1)
        for i, v in enumerate(p):
            shifted[i] = shifted[i] + CENTRE * v
            if i == 0:
                shifted[1] = shifted[1] + SPREAD * v
            else:
                shifted[i - 1] = shifted[i - 1] + 0.5 * SPREAD * v
                shifted[i + 1] = shifted[i + 1] + 0.5 * SPREAD * v
        r = [(r[i] if i < len(r) else zero) - alpha * shifted[i] for i in range(len(shifted))]
        new = form(gram, r)
        beta = new / rr
        p = [r[i] + beta * (p[i] if i < len(p) else zero) for i in range(len(r))]
        rr = new
    return x


def gather_tree(table_rows, across, group):
    found = [
        jnp.take_along_axis(jnp.broadcast_to(one, (8, 128)), across, axis=1, mode="promise_in_bounds")
        for one in table_rows
    ]
    bit = 0
    while len(found) > 1:
        odd = ((group >> bit) & 1) == 1
        found = [jnp.where(odd, found[k + 1], found[k]) for k in range(0, len(found), 2)]
        bit += 1
    return found[0]


def half_turn(tile):
    return pltpu.roll(tile, 4, 0)


def low_half(tile):
    return lax.broadcasted_iota(jnp.int32, tile.shape, 0) < 4


def pack_halos(block, side, corner, fifth):
    for x in range(4):
        near, far = block[x], block[x + 4]
        side[0, x] = jnp.where(low_half(near), near, half_turn(far))
        side[1, x] = jnp.where(low_half(near), half_turn(near), far)
    if fifth:
        for x in range(8):
            side[0, 4, x : x + 1] = block[x, 4:5]
            side[1, 4, x : x + 1] = block[x, 3:4]
    for a in range(2):
        for j in range(2):
            near, far = block[4 * a + j], block[4 * a + 2 + j]
            corner[a, 0, j] = jnp.where(low_half(near), near, half_turn(far))
            corner[a, 1, j] = jnp.where(low_half(near), half_turn(near), far)


def unpack_halos(block, side, dom, corner, wide):
    def put(at, middle, left, right):
        turned = half_turn(middle)
        wide[at, 0:8] = jnp.where(low_half(turned), left, turned)
        wide[at, 8:16] = jnp.where(low_half(turned), turned, right)

    for x in range(8):
        left, right = side[0, x % 4], side[1, x % 4]
        if x < 4:
            right = half_turn(right)
        else:
            left = half_turn(left)
        put(5 + x, block[x], left, right)
    for a in range(2):
        for t in range(5):
            u = t - 1 if a == 0 else t
            if 0 <= u < 4:
                left, right = corner[a, 0, u % 2], corner[a, 1, u % 2]
                if u < 2:
                    right = half_turn(right)
                else:
                    left = half_turn(left)
            else:
                left = right = jnp.zeros((8, 512), F32)
            put(t if a == 0 else 13 + t, dom[a, t], left, right)


def kernel(
    doms,
    slabs,
    heat,
    emitting,
    shift_hbm,
    bucket_hbm,
    factor_hbm,
    rigidity,
    wet_position,
    wet_tally,
    accepting,
    disp,
    spread,
    shift,
    bucket,
    factor,
    heat_pieces,
    slots_out,
    slots_in,
    pieces,
    interp,
    side_out,
    side_in,
    dom_in,
    corner_out,
    corner_in,
    rig_side_out,
    rig_side_in,
    rig_dom_in,
    rig_corner_out,
    rig_corner_in,
    wide,
    rig_wide,
    basis,
    centre,
    dom_moments,
    slab_moments,
    wet_pieces,
    wet_out,
    wet_in,
    load_sem,
    slot_send,
    slot_recv,
    halo_send,
    halo_recv,
    rig_send,
    rig_recv,
    wet_send,
    wet_recv,
    dom_send,
    dom_recv,
    slab_send,
    slab_recv,
):
    d, s = lax.axis_index(DOM), lax.axis_index(SLAB)

    def exists(a, b):
        return (d + a >= 1) & (d + a <= doms) & (s + b >= 1) & (s + b <= slabs)

    loads = [
        pltpu.make_async_copy(src, dst, load_sem.at[i])
        for i, (src, dst) in enumerate(((shift_hbm, shift), (bucket_hbm, bucket), (factor_hbm, factor)))
    ]
    for load in loads:
        load.start()

    barrier = pltpu.get_barrier_semaphore()
    for k in range(1, doms):
        pl.semaphore_signal(barrier, inc=1, device_id=(lax.rem(d + k, doms), s), device_id_type=MESH)
    for k in range(1, slabs):
        pl.semaphore_signal(barrier, inc=1, device_id=(d, lax.rem(s + k, slabs)), device_id_type=MESH)
    expected = doms + slabs - 2
    for a in (0, 2):
        for b in (0, 2):

            @pl.when(exists(a, b))
            def _():
                pl.semaphore_signal(
                    barrier, inc=1, device_id=(d + (a - 1), s + (b - 1)), device_id_type=MESH
                )

            expected = expected + exists(a, b).astype(jnp.int32)

    def halo_copies(block, s_out, s_in, d_in, c_out, c_in, send, recv):
        found = []
        for a in range(3):
            for b in range(3):
                if a == 1 and b == 1:
                    continue
                if a == 1:
                    src, dst = s_out.at[b // 2], s_in.at[1 - b // 2]
                elif b == 1:
                    src, dst = block.at[pl.ds(3 if a == 2 else 0, 5)], d_in.at[1 - a // 2]
                else:
                    src, dst = c_out.at[a // 2, b // 2], c_in.at[1 - a // 2, 1 - b // 2]
                j = 3 * a + b
                copy = pltpu.make_async_remote_copy(
                    src_ref=src,
                    dst_ref=dst,
                    send_sem=send.at[j],
                    recv_sem=recv.at[8 - j],
                    device_id=(d + (a - 1), s + (b - 1)),
                    device_id_type=MESH,
                )
                found.append((a, b, copy))
        return found

    def start_all(copies):
        for a, b, copy in copies:

            @pl.when(exists(a, b))
            def _():
                copy.start()

    def receive_all(copies):
        for a, b, copy in copies:

            @pl.when(exists(2 - a, 2 - b))
            def _():
                copy.wait_recv()

    def finish_all(copies):
        for a, b, copy in copies:

            @pl.when(exists(a, b))
            def _():
                copy.wait_send()

    def clear_missing(s_in, d_in, c_in):
        for a in range(3):
            for b in range(3):
                if a == 1 and b == 1:
                    continue

                @pl.when(jnp.logical_not(exists(a, b)))
                def _():
                    if a == 1:
                        s_in[b // 2] = jnp.zeros((5, 8, 512), F32)
                    elif b == 1:
                        d_in[a // 2] = jnp.zeros((5, 8, 512), F32)
                    else:
                        c_in[a // 2, b // 2] = jnp.zeros((2, 8, 512), F32)

    def clear_blocks(blocks):
        for j in range(9):
            if j == 4:
                continue

            @pl.when(jnp.logical_not(exists(j // 3, j % 3)))
            def _():
                blocks[j] = jnp.zeros(blocks.shape[1:], F32)

    heat_pieces[:64], heat_pieces[64:] = two_pieces(jnp.concatenate([heat[:64], heat[64:]], axis=1))
    pack_halos(rigidity, rig_side_out, rig_corner_out, False)
    for b in range(2):
        rig_side_out[b, 4] = jnp.zeros((8, 512), F32)
    clear_missing(rig_side_in, rig_dom_in, rig_corner_in)
    clear_missing(side_in, dom_in, corner_in)
    clear_blocks(slots_in)
    clear_blocks(wet_in)
    wet_out[...] = jnp.zeros(wet_out.shape, F32)
    rig_copies = halo_copies(
        rigidity, rig_side_out, rig_side_in, rig_dom_in, rig_corner_out, rig_corner_in, rig_send, rig_recv
    )
    def slot_copy(j):
        return pltpu.make_async_remote_copy(
            src_ref=slots_out.at[j],
            dst_ref=slots_in.at[8 - j],
            send_sem=slot_send.at[j],
            recv_sem=slot_recv.at[8 - j],
            device_id=(d + (j // 3 - 1), s + (j % 3 - 1)),
            device_id_type=MESH,
        )

    def start_slot(j):
        @pl.when((j != 4) & exists(j // 3, lax.rem(j, 3)))
        def _():
            slot_copy(j).start()

    def slot_block(t, carry):
        j = lax.rem(t + 5, 9)
        for i in range(16):
            k = jnp.concatenate([emitting[pl.ds(64 * j + 2 * i + r, 1), :] for r in range(2)], axis=1)
            across = (k >> 13) * 128 + (k & 127)
            found = look_up(heat_pieces, 64, across, (k >> 7) & 63)
            found = jnp.sum(found, axis=0, keepdims=True)
            slots_out[j, 2 * i : 2 * i + 1] = found[:, :128]
            slots_out[j, 2 * i + 1 : 2 * i + 2] = found[:, 128:]
        for i in range(4, 8):
            k = emitting[pl.ds(pl.multiple_of(64 * j + 8 * i, 8), 8), :]
            slots_out[j, 8 * i : 8 * i + 8] = gather_tree([heat[r : r + 1] for r in range(128)], k & 127, k >> 7)

        @pl.when(t == 1)
        def _():
            pl.semaphore_wait(barrier, expected)
            start_slot(5)

        @pl.when(t >= 1)
        def _():
            start_slot(j)

        return carry

    lax.fori_loop(0, 9, slot_block, 0)
    start_all(rig_copies)
    slots_in[4] = slots_out[4]
    for load in loads:
        load.wait()
    for j in range(9):
        if j == 4:
            continue

        @pl.when(exists(2 - j // 3, 2 - j % 3))
        def _():
            slot_copy(j).wait_recv()

    for h in range(9):
        table = jnp.concatenate([slots_in[h, :32], slots_in[h, 32:]], axis=1)
        pieces[32 * h : 32 * h + 32], pieces[288 + 32 * h : 320 + 32 * h] = two_pieces(table)

    def matched(k, holder):
        return look_up(pieces, 288, ((k >> 12) & 1) * 128 + (k & 127), holder * 32 + ((k >> 7) & 31))

    def plane(x, carry):
        def rows(half_plane, last):
            for u in range(2):
                q = 2 * half_plane + u

                def pair(ref, corner):
                    ends = [ref[corner, x, pl.ds(2 * q + i, 1), pl.ds(256, 256)] for i in range(2)]
                    return jnp.concatenate([end[:, :128] for end in ends], axis=1)

                for i in range(2):
                    total = jnp.zeros((8, 256), F32)
                    for corner in range(4):
                        at = (corner, x, pl.ds(2 * q + i, 1), pl.ds(0, 256))
                        total = total + matched(bucket[at], shift[at]) * factor[at]
                    interp[x, pl.ds(2 * q + i, 1), pl.ds(0, 256)] = jnp.sum(total, axis=0, keepdims=True)
                total = jnp.zeros((8, 256), F32)
                for corner in range(4):
                    total = total + matched(pair(bucket, corner), pair(shift, corner)) * pair(factor, corner)
                total = jnp.sum(total, axis=0, keepdims=True)
                for i in range(2):
                    both = jnp.concatenate([total[:, 128 * i : 128 * i + 128]] * 2, axis=1)
                    interp[x, pl.ds(2 * q + i, 1), pl.ds(256, 256)] = both

                at = (q, x, slice(None), pl.ds(384, 128))
                k, holder = bucket[at], shift[at]
                found = None
                for h in range(9):
                    one = gather_tree([slots_in[h, r : r + 1] for r in range(64)], k & 127, k >> 7)
                    found = one if found is None else jnp.where(holder == h, one, found)
                last = last + factor[at] * found
            return last

        interp[x, :, 384:512] = lax.fori_loop(0, 2, rows, jnp.zeros((8, 128), F32))
        return carry

    lax.fori_loop(0, 8, plane, 0)

    pack_halos(interp, side_out, corner_out, True)
    copies = halo_copies(interp, side_out, side_in, dom_in, corner_out, corner_in, halo_send, halo_recv)
    start_all(copies)
    receive_all(rig_copies)
    unpack_halos(rigidity, rig_side_in, rig_dom_in, rig_corner_in, rig_wide)
    receive_all(copies)
    unpack_halos(interp, side_in, dom_in, corner_in, wide)

    row = lax.broadcasted_iota(jnp.int32, (16, 512), 0)
    lane = lax.broadcasted_iota(jnp.int32, (16, 512), 1)
    row_inside = ((row >= 4) | (s > 0)) & ((row < 12) | (s < slabs - 1))

    def inside(xx):
        return row_inside & ((xx >= 4) | (d > 0)) & ((xx < 12) | (d < doms - 1))

    def back_z(v):
        return jnp.where(lane == 0, 0.0, pltpu.roll(v, 1, 1))

    def ahead_z(v):
        return jnp.where(lane == 511, 0.0, pltpu.roll(v, 511, 1))

    def load_plane(xx, carry):
        here = wide[xx + 1]
        keep = inside(xx)
        at = jnp.clip(xx - 4, 0, 7)
        back = jnp.where(row == 0, side_in[0, 4, pl.ds(at, 1), :], pltpu.roll(here, 1, 0))
        ahead = jnp.where(row == 15, side_in[1, 4, pl.ds(at, 1), :], pltpu.roll(here, 15, 0))
        basis[0, 0, xx] = jnp.where(keep, COEF * (wide[xx + 2] - wide[xx]), 0.0)
        basis[0, 1, xx] = jnp.where(keep, COEF * (ahead - back), 0.0)
        basis[0, 2, xx] = jnp.where(keep, COEF * (ahead_z(here) - back_z(here)), 0.0)
        return carry

    lax.fori_loop(0, 16, load_plane, 0)

    def scaled_operate(level, c, xx):
        v = basis[level, c, xx]
        beside = basis[level, c, xx - 1] + basis[level, c, xx + 1]
        beside = beside + pltpu.roll(v, 1, 0) + pltpu.roll(v, 15, 0)
        beside = beside + back_z(v) + ahead_z(v)
        return ((rig_wide[xx + 1] + (6.0 - CENTRE)) * v - beside) * (1.0 / SPREAD)

    for level in range(1, 4):

        def next_plane(xx, carry, level=level):
            keep = inside(xx)
            for c in range(3):
                image = scaled_operate(level - 1, c, xx)
                if level > 1:
                    image = 2.0 * image - basis[level - 2, c, xx]
                basis[level, c, xx] = jnp.where(keep, image, 0.0)
            return carry

        lax.fori_loop(level, 16 - level, next_plane, 0)

    def folded(field):
        return jnp.where(low_half(field[:8]), field[8:], field[:8])

    def moment_plane(xx, totals):
        totals = list(totals)
        for c in range(3):
            w = [folded(basis[level, c, xx]) for level in range(4)]
            for level in range(4):
                centre[level, c, xx - 4] = w[level]
            w.append(folded(scaled_operate(3, c, xx)))
            pairs = ((0, 0), (0, 1), (1, 1), (1, 2), (2, 2), (2, 3), (3, 3), (3, 4))
            for i, (one, two) in enumerate(pairs):
                product = w[one] * w[two]
                product = (product[:, :128] + product[:, 128:256]) + (product[:, 256:384] + product[:, 384:])
                totals[i] = totals[i] + product
        return tuple(totals)

    totals = lax.fori_loop(4, 12, moment_plane, tuple(jnp.zeros((8, 128), F32) for _ in range(8)))
    for i in range(8):
        dom_moments[0, i : i + 1] = jnp.sum(totals[i], axis=0, keepdims=True)

    def reduce_copy(buffer, send, recv, source, target, device):
        return pltpu.make_async_remote_copy(
            src_ref=buffer.at[source],
            dst_ref=buffer.at[target],
            send_sem=send,
            recv_sem=recv,
            device_id=device,
            device_id_type=MESH,
        )

    for k in range(1, doms):
        reduce_copy(dom_moments, dom_send, dom_recv, 0, k, (lax.rem(d + k, doms), s)).start()
    others = pl.ds(1, doms - 1)
    dom_all = reduce_copy(dom_moments, dom_send, dom_recv, others, others, (lax.rem(d + 1, doms), s))
    others = pl.ds(1, slabs - 1)
    slab_all = reduce_copy(slab_moments, slab_send, slab_recv, others, others, (d, lax.rem(s + 1, slabs)))

    for level in range(4):
        for c in range(3):
            for x in range(8):
                for half in range(2):
                    high, low = two_pieces(centre[level, c, x, :, 256 * half : 256 * half + 256])
                    at = 16 * x + 8 * half
                    at = at + 256 * (3 * level + c)
                    wet_pieces[at : at + 8] = high
                    wet_pieces[128 + at : 136 + at] = low

    def wet_block(a):
        node = jnp.concatenate([wet_position[3 * a + b] for b in range(3)], axis=1)
        group = (node >> 12) * 16 + ((node >> 8) & 1) * 8 + (((node >> 9) + 4) & 7)
        slot = lax.broadcasted_iota(jnp.int32, (1, 128), 1)
        live = jnp.concatenate(
            [slot < wet_tally[0:1, 3 * a + b : 3 * a + b + 1] for b in range(3)], axis=1
        )
        picked = jnp.dot(wet_pieces[...], one_hot(node & 255), preferred_element_type=F32)
        for kc in range(12):
            found = pick_group(picked[256 * kc : 256 * kc + 256], 128, group)
            found = jnp.where(live, jnp.sum(found, axis=0, keepdims=True), 0.0)
            at = kc // 3 * 4 + kc % 3
            for b in range(3):
                wet_out[3 * a + b, at : at + 1] = found[:, 128 * b : 128 * b + 128]

    wet_block(0)
    dom_all.wait_recv()
    total = dom_moments[0]
    for k in range(1, doms):
        total = total + dom_moments[k]
    slab_moments[0] = total
    for k in range(1, slabs):
        reduce_copy(slab_moments, slab_send, slab_recv, 0, k, (d, lax.rem(s + k, slabs))).start()
    wet_block(1)
    wet_block(2)

    wet_copies = []
    for j in range(9):
        if j == 4:
            continue
        copy = pltpu.make_async_remote_copy(
            src_ref=wet_out.at[j],
            dst_ref=wet_in.at[8 - j],
            send_sem=wet_send.at[j],
            recv_sem=wet_recv.at[8 - j],
            device_id=(d + (j // 3 - 1), s + (j % 3 - 1)),
            device_id_type=MESH,
        )
        wet_copies.append((j // 3, j % 3, copy))
    start_all(wet_copies)
    wet_in[4] = wet_out[4]

    taker = jnp.concatenate([accepting[j] for j in range(9)], axis=1)
    lane_of = lax.broadcasted_iota(jnp.int32, (128, 1152), 0)
    lane_hot = jnp.where(lane_of == (taker & 127), 1.0, 0.0).astype(BF16)

    slab_all.wait_recv()
    total = slab_moments[0]
    for k in range(1, slabs):
        total = total + slab_moments[k]
    c = coefficients([jnp.sum(total[i : i + 1], axis=1, keepdims=True) for i in range(8)])

    def combine(x, carry):
        for a in range(3):
            field = c[0] * centre[0, a, x]
            for level in range(1, 4):
                field = field + c[level] * centre[level, a, x]
            disp[a, x] = half_turn(field)
        return carry

    lax.fori_loop(0, 8, combine, 0)

    receive_all(wet_copies)
    sub = lax.broadcasted_iota(jnp.int32, (8, 1), 0)
    first = jnp.where(sub < 4, c[0], c[1])
    second = jnp.where(sub < 4, c[2], c[3])
    value = jnp.concatenate([wet_in[j, :8] * first + wet_in[j, 8:] * second for j in range(9)], axis=1)
    value = value + half_turn(value)
    high = value.astype(BF16).astype(F32)
    apart = (taker >> 7) - (lax.broadcasted_iota(jnp.int32, (8, 1152), 0) >> 2)
    for part_of in range(4):
        at = range(16 * part_of, 16 * part_of + 16)
        lines = [
            jnp.where(apart == 2 * h, part, 0.0).astype(BF16) for part in (high, value - high) for h in at
        ]
        put = lax.dot_general(
            jnp.concatenate(lines, axis=0), lane_hot, (((1,), (1,)), ((), ())), preferred_element_type=F32
        )
        spread[128 * part_of : 128 * part_of + 128] = put[:128] + put[128:]

    finish_all(rig_copies)
    for j in range(9):
        if j == 4:
            continue

        @pl.when(exists(j // 3, j % 3))
        def _():
            slot_copy(j).wait_send()

    finish_all(copies)
    finish_all(wet_copies)
    dom_all.wait_send()
    slab_all.wait_send()


def on_device(doms, slabs, heat, emitting, shift, bucket, factor, rigidity, position, tally, accepting):
    dma = pltpu.SemaphoreType.DMA
    vm = pltpu.VMEM
    halos_out = [vm((2, 5, 8, 512), F32), vm((2, 2, 2, 8, 512), F32)]
    halos_in = [vm((2, 5, 8, 512), F32), vm((2, 5, 8, 512), F32), vm((2, 2, 2, 8, 512), F32)]
    halos = [halos_out[0], halos_in[0], halos_in[1], halos_out[1], halos_in[2]]
    whole = pl.BlockSpec(memory_space=pltpu.VMEM)
    away = pl.BlockSpec(memory_space=pl.ANY)
    disp, spread = pl.pallas_call(
        functools.partial(kernel, doms, slabs),
        out_shape=[
            jax.ShapeDtypeStruct((3, 8, 8, 512), F32),
            jax.ShapeDtypeStruct((512, 128), F32),
        ],
        in_specs=[whole, whole, away, away, away, whole, whole, whole, whole],
        out_specs=[whole, whole],
        scratch_shapes=[
            vm((4, 8, 8, 512), jnp.int32),
            vm((4, 8, 8, 512), jnp.int32),
            vm((4, 8, 8, 512), F32),
            vm((128, 256), BF16),
            vm((9, 64, 128), F32),
            vm((9, 64, 128), F32),
            vm((576, 256), BF16),
            vm((8, 8, 512), F32),
            *halos,
            *halos,
            vm((18, 16, 512), F32),
            vm((18, 16, 512), F32),
            vm((4, 3, 16, 16, 512), F32),
            vm((4, 3, 8, 8, 512), F32),
            vm((doms, 8, 128), F32),
            vm((slabs, 8, 128), F32),
            vm((3072, 256), BF16),
            vm((9, 16, 128), F32),
            vm((9, 16, 128), F32),
            dma((3,)),
            dma((9,)),
            dma((9,)),
            dma((9,)),
            dma((9,)),
            dma((9,)),
            dma((9,)),
            dma((9,)),
            dma((9,)),
            dma,
            dma,
            dma,
            dma,
        ],
        compiler_params=pltpu.CompilerParams(
            collective_id=0, has_side_effects=True, vmem_limit_bytes=56 * 2**20
        ),
    )(
        heat.reshape(128, 128),
        emitting.reshape(576, 128),
        shift,
        bucket,
        factor,
        rigidity,
        position.reshape(9, 1, 128),
        tally,
        accepting.reshape(9, 1, 128),
    )
    spread = spread.reshape(128, 4, 128)[:, :3]
    return disp, spread.transpose(1, 0, 2).reshape(3, -1)


def solution(mesh):
    in_specs = (
        P(BOTH),
        P(BOTH, None, None, None),
        P(None, DOM, SLAB, None),
        P(None, DOM, SLAB, None),
        P(None, DOM, SLAB, None),
        P(DOM, SLAB, None),
        P(BOTH, None, None, None),
        P(BOTH, None),
        P(BOTH, None, None, None),
    )
    out_specs = (P(None, DOM, SLAB, None), P(None, BOTH))
    return jax.shard_map(
        functools.partial(on_device, mesh.shape[DOM], mesh.shape[SLAB]),
        mesh=mesh,
        in_specs=in_specs,
        out_specs=out_specs,
        check_vma=False,
    )
```

```python
import functools

import jax
import jax.numpy as jnp
from jax import lax
from jax.experimental import pallas as pl
from jax.experimental.pallas import tpu as pltpu
from jax.sharding import PartitionSpec as P

DOM = "dom"
SLAB = "slab"
BOTH = ("dom", "slab")
MESH = pl.DeviceIdType.MESH
ITERS = 4
COEF = 0.5
CENTRE = 7.125
SPREAD = 6.875
F32 = jnp.float32
BF16 = jnp.bfloat16


def two_pieces(table):
    high = table.astype(BF16)
    low = (table - high.astype(F32)).astype(BF16)
    return high, low


def one_hot(across):
    width = across.shape[1]
    hot = lax.broadcasted_iota(jnp.int32, (256, width), 0) == across
    return jnp.where(hot, 1.0, 0.0).astype(BF16)


def pick_group(picked, groups, group):
    width = group.shape[1]
    picked = picked[:groups] + picked[groups:]
    apart = group - lax.broadcasted_iota(jnp.int32, (8, width), 0)
    total = jnp.zeros((8, width), F32)
    for k in range(groups // 8):
        total = jnp.where(apart == 8 * k, picked[8 * k : 8 * k + 8], total)
    return total


def look_up(pieces_ref, groups, across, group):
    picked = jnp.dot(pieces_ref[...], one_hot(across), preferred_element_type=F32)
    return pick_group(picked, groups, group)


def coefficients(moments):
    m = list(moments[:7])
    m[2], m[3] = 2.0 * m[2] - m[0], 2.0 * m[3] - m[1]
    m[4], m[5], m[6] = 2.0 * m[4] - m[0], 2.0 * m[5] - m[1], 2.0 * m[6] - m[0]
    gram = [[0.5 * (m[i + j] + m[abs(i - j)]) for j in range(4)] for i in range(4)]
    h = [[None] * 4 for _ in range(4)]
    for i in range(4):
        h[i][0] = gram[i][1]
        h[i][1] = 0.5 * (gram[i][0] + gram[i][2])
        h[i][2] = 0.5 * (gram[i][1] + gram[i][3])
    for i in range(3):
        h[i][3] = h[3][i]
    h[3][3] = moments[7]
    image = [[CENTRE * gram[i][j] + SPREAD * h[i][j] for j in range(4)] for i in range(4)]

    def form(matrix, v):
        n = len(v)
        return sum(
            (matrix[i][j] if i == j else 2.0 * matrix[i][j]) * v[i] * v[j]
            for i in range(n)
            for j in range(i, n)
        )

    one = jnp.ones_like(m[0])
    zero = jnp.zeros_like(m[0])
    x, r, p = [], [one], [one]
    rr = form(gram, r)
    for step in range(ITERS):
        alpha = rr / form(image, p)
        x = [(x[i] if i < len(x) else zero) + alpha * p[i] for i in range(len(p))]
        if step + 1 == ITERS:
            break
        shifted = [zero] * (len(p) + 1)
        for i, v in enumerate(p):
            shifted[i] = shifted[i] + CENTRE * v
            if i == 0:
                shifted[1] = shifted[1] + SPREAD * v
            else:
                shifted[i - 1] = shifted[i - 1] + 0.5 * SPREAD * v
                shifted[i + 1] = shifted[i + 1] + 0.5 * SPREAD * v
        r = [(r[i] if i < len(r) else zero) - alpha * shifted[i] for i in range(len(shifted))]
        new = form(gram, r)
        beta = new / rr
        p = [r[i] + beta * (p[i] if i < len(p) else zero) for i in range(len(r))]
        rr = new
    return x


def gather_tree(table_rows, across, group):
    found = [
        jnp.take_along_axis(jnp.broadcast_to(one, (8, 128)), across, axis=1, mode="promise_in_bounds")
        for one in table_rows
    ]
    bit = 0
    while len(found) > 1:
        odd = ((group >> bit) & 1) == 1
        found = [jnp.where(odd, found[k + 1], found[k]) for k in range(0, len(found), 2)]
        bit += 1
    return found[0]


def half_turn(tile):
    return pltpu.roll(tile, 4, 0)


def low_half(tile):
    return lax.broadcasted_iota(jnp.int32, tile.shape, 0) < 4


def pack_pair(near, far):
    return (
        jnp.where(low_half(near), near, half_turn(far)),
        jnp.where(low_half(near), half_turn(near), far),
    )


def pack_halos(block, side, corner):
    for x in range(4):
        side[0, x], side[1, x] = pack_pair(block[x], block[x + 4])
    for a in range(2):
        for j in range(2):
            corner[a, 0, j], corner[a, 1, j] = pack_pair(block[4 * a + j], block[4 * a + 2 + j])


def unpack_halos(block, side, dom, corner, wide):
    def put(at, middle, left, right):
        turned = half_turn(middle)
        wide[at, 0:8] = jnp.where(low_half(turned), left, turned)
        wide[at, 8:16] = jnp.where(low_half(turned), turned, right)

    for x in range(8):
        left, right = side[0, x % 4], side[1, x % 4]
        if x < 4:
            right = half_turn(right)
        else:
            left = half_turn(left)
        put(5 + x, block[x], left, right)
    for a in range(2):
        for t in range(5):
            u = t - 1 if a == 0 else t
            if 0 <= u < 4:
                left, right = corner[a, 0, u % 2], corner[a, 1, u % 2]
                if u < 2:
                    right = half_turn(right)
                else:
                    left = half_turn(left)
            else:
                left = right = jnp.zeros((8, 512), F32)
            put(t if a == 0 else 13 + t, dom[a, t], left, right)


def kernel(
    doms,
    slabs,
    heat,
    emitting,
    shift_hbm,
    bucket_hbm,
    factor_hbm,
    rigidity,
    wet_position,
    wet_tally,
    accepting,
    disp,
    spread,
    shift,
    bucket,
    factor,
    heat_pieces,
    slots_out,
    slots_in,
    pieces,
    interp,
    side_out,
    side_in,
    dom_in,
    corner_out,
    corner_in,
    rig_side_out,
    rig_side_in,
    rig_dom_in,
    rig_corner_out,
    rig_corner_in,
    wide,
    rig_wide,
    basis_0,
    basis_1,
    basis_2,
    basis_3,
    centre,
    dom_moments,
    slab_moments,
    wet_pieces,
    wet_out,
    wet_in,
    load_sem,
    slot_send,
    slot_recv,
    halo_send,
    halo_recv,
    rig_send,
    rig_recv,
    wet_send,
    wet_recv,
    dom_send,
    dom_recv,
    slab_send,
    slab_recv,
):
    d, s = lax.axis_index(DOM), lax.axis_index(SLAB)

    def exists(a, b):
        return (d + a >= 1) & (d + a <= doms) & (s + b >= 1) & (s + b <= slabs)

    loads = [
        pltpu.make_async_copy(src, dst, load_sem.at[i])
        for i, (src, dst) in enumerate(((shift_hbm, shift), (bucket_hbm, bucket), (factor_hbm, factor)))
    ]
    for load in loads:
        load.start()

    barrier = pltpu.get_barrier_semaphore()
    for k in range(1, doms):
        pl.semaphore_signal(barrier, inc=1, device_id=(lax.rem(d + k, doms), s), device_id_type=MESH)
    for k in range(1, slabs):
        pl.semaphore_signal(barrier, inc=1, device_id=(d, lax.rem(s + k, slabs)), device_id_type=MESH)
    expected = doms + slabs - 2
    for a in (0, 2):
        for b in (0, 2):

            @pl.when(exists(a, b))
            def _():
                pl.semaphore_signal(
                    barrier, inc=1, device_id=(d + (a - 1), s + (b - 1)), device_id_type=MESH
                )

            expected = expected + exists(a, b).astype(jnp.int32)

    def halo_copies(block, s_out, s_in, d_in, c_out, c_in, send, recv):
        found = []
        for a in range(3):
            for b in range(3):
                if a == 1 and b == 1:
                    continue
                if a == 1:
                    src, dst = s_out.at[b // 2], s_in.at[1 - b // 2]
                elif b == 1:
                    src, dst = block.at[pl.ds(3 if a == 2 else 0, 5)], d_in.at[1 - a // 2]
                else:
                    src, dst = c_out.at[a // 2, b // 2], c_in.at[1 - a // 2, 1 - b // 2]
                j = 3 * a + b
                copy = pltpu.make_async_remote_copy(
                    src_ref=src,
                    dst_ref=dst,
                    send_sem=send.at[j],
                    recv_sem=recv.at[8 - j],
                    device_id=(d + (a - 1), s + (b - 1)),
                    device_id_type=MESH,
                )
                found.append((a, b, copy))
        return found

    def start_all(copies):
        for a, b, copy in copies:

            @pl.when(exists(a, b))
            def _():
                copy.start()

    def receive_all(copies):
        for a, b, copy in copies:

            @pl.when(exists(2 - a, 2 - b))
            def _():
                copy.wait_recv()

    def finish_all(copies):
        for a, b, copy in copies:

            @pl.when(exists(a, b))
            def _():
                copy.wait_send()

    def clear_missing(s_in, d_in, c_in):
        for a in range(3):
            for b in range(3):
                if a == 1 and b == 1:
                    continue

                @pl.when(jnp.logical_not(exists(a, b)))
                def _():
                    if a == 1:
                        s_in[b // 2] = jnp.zeros((5, 8, 512), F32)
                    elif b == 1:
                        d_in[a // 2] = jnp.zeros((5, 8, 512), F32)
                    else:
                        c_in[a // 2, b // 2] = jnp.zeros((2, 8, 512), F32)

    def clear_blocks(blocks):
        for j in range(9):
            if j == 4:
                continue

            @pl.when(jnp.logical_not(exists(j // 3, j % 3)))
            def _():
                blocks[j] = jnp.zeros(blocks.shape[1:], F32)

    heat_pieces[:64], heat_pieces[64:] = two_pieces(jnp.concatenate([heat[:64], heat[64:]], axis=1))
    clear_missing(rig_side_in, rig_dom_in, rig_corner_in)
    clear_missing(side_in, dom_in, corner_in)
    clear_blocks(slots_in)
    clear_blocks(wet_in)
    wet_out[...] = jnp.zeros(wet_out.shape, F32)
    rig_copies = halo_copies(
        rigidity, rig_side_out, rig_side_in, rig_dom_in, rig_corner_out, rig_corner_in, rig_send, rig_recv
    )
    def slot_copy(j):
        return pltpu.make_async_remote_copy(
            src_ref=slots_out.at[j],
            dst_ref=slots_in.at[8 - j],
            send_sem=slot_send.at[j],
            recv_sem=slot_recv.at[8 - j],
            device_id=(d + (j // 3 - 1), s + (j % 3 - 1)),
            device_id_type=MESH,
        )

    def start_slot(j):
        @pl.when((j != 4) & exists(j // 3, lax.rem(j, 3)))
        def _():
            slot_copy(j).start()

    def slot_block(t, carry):
        j = lax.rem(t + 5, 9)
        for i in range(16):
            k = jnp.concatenate([emitting[pl.ds(64 * j + 2 * i + r, 1), :] for r in range(2)], axis=1)
            across = (k >> 13) * 128 + (k & 127)
            found = look_up(heat_pieces, 64, across, (k >> 7) & 63)
            found = jnp.sum(found, axis=0, keepdims=True)
            slots_out[j, 2 * i : 2 * i + 1] = found[:, :128]
            slots_out[j, 2 * i + 1 : 2 * i + 2] = found[:, 128:]
        for i in range(4, 8):
            k = emitting[pl.ds(pl.multiple_of(64 * j + 8 * i, 8), 8), :]
            slots_out[j, 8 * i : 8 * i + 8] = gather_tree([heat[r : r + 1] for r in range(128)], k & 127, k >> 7)

        @pl.when(t == 3)
        def _():
            pl.semaphore_wait(barrier, expected)
            for early in (5, 6, 7):
                start_slot(jnp.int32(early))

        @pl.when(t >= 3)
        def _():
            start_slot(j)

        return carry

    lax.fori_loop(0, 9, slot_block, 0)
    pack_halos(rigidity, rig_side_out, rig_corner_out)
    for b in range(2):
        rig_side_out[b, 4] = jnp.zeros((8, 512), F32)
    start_all(rig_copies)
    slots_in[4] = slots_out[4]
    for load in loads:
        load.wait()
    for j in range(9):
        if j == 4:
            continue

        @pl.when(exists(2 - j // 3, 2 - j % 3))
        def _():
            slot_copy(j).wait_recv()

    for h in range(9):
        table = jnp.concatenate([slots_in[h, :32], slots_in[h, 32:]], axis=1)
        pieces[32 * h : 32 * h + 32], pieces[288 + 32 * h : 320 + 32 * h] = two_pieces(table)

    def matched(k, holder):
        return look_up(pieces, 288, ((k >> 12) & 1) * 128 + (k & 127), holder * 32 + ((k >> 7) & 31))

    def plane(x, carry):
        def rows(half_plane, last):
            for u in range(2):
                q = 2 * half_plane + u

                def pair(ref, corner):
                    ends = [ref[corner, x, pl.ds(2 * q + i, 1), pl.ds(256, 256)] for i in range(2)]
                    return jnp.concatenate([end[:, :128] for end in ends], axis=1)

                for i in range(2):
                    total = jnp.zeros((8, 256), F32)
                    for corner in range(4):
                        at = (corner, x, pl.ds(2 * q + i, 1), pl.ds(0, 256))
                        total = total + matched(bucket[at], shift[at]) * factor[at]
                    interp[x, pl.ds(2 * q + i, 1), pl.ds(0, 256)] = jnp.sum(total, axis=0, keepdims=True)
                total = jnp.zeros((8, 256), F32)
                for corner in range(4):
                    total = total + matched(pair(bucket, corner), pair(shift, corner)) * pair(factor, corner)
                total = jnp.sum(total, axis=0, keepdims=True)
                for i in range(2):
                    both = jnp.concatenate([total[:, 128 * i : 128 * i + 128]] * 2, axis=1)
                    interp[x, pl.ds(2 * q + i, 1), pl.ds(256, 256)] = both

                at = (q, x, slice(None), pl.ds(384, 128))
                k, holder = bucket[at], shift[at]
                found = None
                for h in range(9):
                    one = gather_tree([slots_in[h, r : r + 1] for r in range(64)], k & 127, k >> 7)
                    found = one if found is None else jnp.where(holder == h, one, found)
                last = last + factor[at] * found
            return last

        interp[x, :, 384:512] = lax.fori_loop(0, 2, rows, jnp.zeros((8, 128), F32))
        return carry

    copies = halo_copies(interp, side_out, side_in, dom_in, corner_out, corner_in, halo_send, halo_recv)

    def send_piece(a, b, src, dst):
        j = 3 * a + b

        @pl.when(exists(a, b))
        def _():
            pltpu.make_async_remote_copy(
                src_ref=src,
                dst_ref=dst,
                send_sem=halo_send.at[j],
                recv_sem=halo_recv.at[8 - j],
                device_id=(d + (a - 1), s + (b - 1)),
                device_id_type=MESH,
            ).start()

    def plane_pair(q, carry):
        p = lax.rem(2 * q, 4) + q // 2
        lax.fori_loop(0, 2, lambda e, carry: plane(p + 4 * e, carry), 0)
        near, far = interp[p], interp[p + 4]
        side_out[0, p], side_out[1, p] = pack_pair(near, far)
        for b in range(2):
            side_out[b, 4, pl.ds(p, 1), :] = near[4 - b : 5 - b]
            side_out[b, 4, pl.ds(p + 4, 1), :] = far[4 - b : 5 - b]
            send_piece(1, 2 * b, side_out.at[b, p], side_in.at[1 - b, p])
        send_piece(0, 1, interp.at[p], dom_in.at[1, p])
        send_piece(2, 1, interp.at[p + 4], dom_in.at[0, p + 1])

        @pl.when(q == 0)
        def _():
            send_piece(0, 1, interp.at[4], dom_in.at[1, 4])

        @pl.when(q % 2 == 1)
        def _():
            j = q // 2
            for a in range(2):
                pieces_of = pack_pair(interp[4 * a + j], interp[4 * a + 2 + j])
                for b in range(2):
                    corner_out[a, b, j] = pieces_of[b]
                    send_piece(2 * a, 2 * b, corner_out.at[a, b, j], corner_in.at[1 - a, 1 - b, j])

        @pl.when(q == 3)
        def _():
            send_piece(2, 1, interp.at[3], dom_in.at[0, 0])
            for b in range(2):
                send_piece(1, 2 * b, side_out.at[b, 4], side_in.at[1 - b, 4])

        return carry

    lax.fori_loop(0, 4, plane_pair, 0)

    receive_all(rig_copies)
    unpack_halos(rigidity, rig_side_in, rig_dom_in, rig_corner_in, rig_wide)
    receive_all(copies)
    unpack_halos(interp, side_in, dom_in, corner_in, wide)

    row = lax.broadcasted_iota(jnp.int32, (16, 512), 0)
    lane = lax.broadcasted_iota(jnp.int32, (16, 512), 1)
    row_inside = ((row >= 4) | (s > 0)) & ((row < 12) | (s < slabs - 1))

    def inside(xx):
        return row_inside & ((xx >= 4) | (d > 0)) & ((xx < 12) | (d < doms - 1))

    def back_z(v):
        return jnp.where(lane == 0, 0.0, pltpu.roll(v, 1, 1))

    def ahead_z(v):
        return jnp.where(lane == 511, 0.0, pltpu.roll(v, 511, 1))

    basis = (basis_0, basis_1, basis_2, basis_3)

    def by_twos(first, end, body, carry):
        def two(i, carry):
            return body(first + 2 * i + 1, body(first + 2 * i, carry))

        return lax.fori_loop(0, (end - first) // 2, two, carry)

    def load_plane(xx, carry):
        here = wide[xx + 1]
        keep = inside(xx)
        at = jnp.clip(xx - 4, 0, 7)
        back = jnp.where(row == 0, side_in[0, 4, pl.ds(at, 1), :], pltpu.roll(here, 1, 0))
        ahead = jnp.where(row == 15, side_in[1, 4, pl.ds(at, 1), :], pltpu.roll(here, 15, 0))
        basis_0[0, xx] = jnp.where(keep, COEF * (wide[xx + 2] - wide[xx]), 0.0)
        basis_0[1, xx] = jnp.where(keep, COEF * (ahead - back), 0.0)
        basis_0[2, xx] = jnp.where(keep, COEF * (ahead_z(here) - back_z(here)), 0.0)
        return carry

    by_twos(0, 16, load_plane, 0)

    def scaled_operate(level, c, xx):
        v = basis[level][c, xx]
        beside = basis[level][c, xx - 1] + basis[level][c, xx + 1]
        beside = beside + pltpu.roll(v, 1, 0) + pltpu.roll(v, 15, 0)
        beside = beside + back_z(v) + ahead_z(v)
        return ((rig_wide[xx + 1] + (6.0 - CENTRE)) * v - beside) * (1.0 / SPREAD)

    for level in range(1, 4):

        def next_plane(xx, carry, level=level):
            keep = inside(xx)
            for c in range(3):
                image = scaled_operate(level - 1, c, xx)
                if level > 1:
                    image = 2.0 * image - basis[level - 2][c, xx]
                basis[level][c, xx] = jnp.where(keep, image, 0.0)
            return carry

        by_twos(level, 16 - level, next_plane, 0)

    def folded(field):
        return jnp.where(low_half(field[:8]), field[8:], field[:8])

    def moment_plane(xx, totals):
        totals = list(totals)
        for c in range(3):
            w = [folded(basis[level][c, xx]) for level in range(4)]
            for level in range(4):
                centre[level, c, xx - 4] = w[level]
            w.append(folded(scaled_operate(3, c, xx)))
            pairs = ((0, 0), (0, 1), (1, 1), (1, 2), (2, 2), (2, 3), (3, 3), (3, 4))
            for i, (one, two) in enumerate(pairs):
                product = w[one] * w[two]
                product = (product[:, :128] + product[:, 128:256]) + (product[:, 256:384] + product[:, 384:])
                totals[i] = totals[i] + product
        return tuple(totals)

    totals = by_twos(4, 12, moment_plane, tuple(jnp.zeros((8, 128), F32) for _ in range(8)))
    for i in range(8):
        dom_moments[0, i : i + 1] = jnp.sum(totals[i], axis=0, keepdims=True)

    def reduce_copy(buffer, send, recv, source, target, device):
        return pltpu.make_async_remote_copy(
            src_ref=buffer.at[source],
            dst_ref=buffer.at[target],
            send_sem=send,
            recv_sem=recv,
            device_id=device,
            device_id_type=MESH,
        )

    for k in range(1, doms):
        reduce_copy(dom_moments, dom_send, dom_recv, 0, k, (lax.rem(d + k, doms), s)).start()
    others = pl.ds(1, doms - 1)
    dom_all = reduce_copy(dom_moments, dom_send, dom_recv, others, others, (lax.rem(d + 1, doms), s))
    others = pl.ds(1, slabs - 1)
    slab_all = reduce_copy(slab_moments, slab_send, slab_recv, others, others, (d, lax.rem(s + 1, slabs)))

    for level in range(4):
        for c in range(3):
            for x in range(8):
                for half in range(2):
                    high, low = two_pieces(centre[level, c, x, :, 256 * half : 256 * half + 256])
                    at = 16 * x + 8 * half
                    at = at + 256 * (3 * level + c)
                    wet_pieces[at : at + 8] = high
                    wet_pieces[128 + at : 136 + at] = low

    def wet_block(a):
        node = jnp.concatenate([wet_position[3 * a + b] for b in range(3)], axis=1)
        group = (node >> 12) * 16 + ((node >> 8) & 1) * 8 + (((node >> 9) + 4) & 7)
        slot = lax.broadcasted_iota(jnp.int32, (1, 128), 1)
        live = jnp.concatenate(
            [slot < wet_tally[0:1, 3 * a + b : 3 * a + b + 1] for b in range(3)], axis=1
        )
        picked = jnp.dot(wet_pieces[...], one_hot(node & 255), preferred_element_type=F32)
        for kc in range(12):
            found = pick_group(picked[256 * kc : 256 * kc + 256], 128, group)
            found = jnp.where(live, jnp.sum(found, axis=0, keepdims=True), 0.0)
            at = kc // 3 * 4 + kc % 3
            for b in range(3):
                wet_out[3 * a + b, at : at + 1] = found[:, 128 * b : 128 * b + 128]

    wet_block(0)
    dom_all.wait_recv()
    total = dom_moments[0]
    for k in range(1, doms):
        total = total + dom_moments[k]
    slab_moments[0] = total
    for k in range(1, slabs):
        reduce_copy(slab_moments, slab_send, slab_recv, 0, k, (d, lax.rem(s + k, slabs))).start()
    wet_block(1)
    wet_block(2)

    wet_copies = []
    for j in range(9):
        if j == 4:
            continue
        copy = pltpu.make_async_remote_copy(
            src_ref=wet_out.at[j],
            dst_ref=wet_in.at[8 - j],
            send_sem=wet_send.at[j],
            recv_sem=wet_recv.at[8 - j],
            device_id=(d + (j // 3 - 1), s + (j % 3 - 1)),
            device_id_type=MESH,
        )
        wet_copies.append((j // 3, j % 3, copy))
    start_all(wet_copies)
    wet_in[4] = wet_out[4]

    taker = jnp.concatenate([accepting[j] for j in range(9)], axis=1)
    lane_of = lax.broadcasted_iota(jnp.int32, (128, 1152), 0)
    lane_hot = jnp.where(lane_of == (taker & 127), 1.0, 0.0).astype(BF16)

    slab_all.wait_recv()
    total = slab_moments[0]
    for k in range(1, slabs):
        total = total + slab_moments[k]
    c = coefficients([jnp.sum(total[i : i + 1], axis=1, keepdims=True) for i in range(8)])

    def combine(x, carry):
        for a in range(3):
            field = c[0] * centre[0, a, x]
            for level in range(1, 4):
                field = field + c[level] * centre[level, a, x]
            disp[a, x] = half_turn(field)
        return carry

    lax.fori_loop(0, 8, combine, 0)

    receive_all(wet_copies)
    sub = lax.broadcasted_iota(jnp.int32, (8, 1), 0)
    first = jnp.where(sub < 4, c[0], c[1])
    second = jnp.where(sub < 4, c[2], c[3])
    value = jnp.concatenate([wet_in[j, :8] * first + wet_in[j, 8:] * second for j in range(9)], axis=1)
    value = value + half_turn(value)
    high = value.astype(BF16).astype(F32)
    apart = (taker >> 7) - (lax.broadcasted_iota(jnp.int32, (8, 1152), 0) >> 2)
    for part_of in range(4):
        at = range(16 * part_of, 16 * part_of + 16)
        lines = [
            jnp.where(apart == 2 * h, part, 0.0).astype(BF16) for part in (high, value - high) for h in at
        ]
        put = lax.dot_general(
            jnp.concatenate(lines, axis=0), lane_hot, (((1,), (1,)), ((), ())), preferred_element_type=F32
        )
        put = put[:128] + put[128:]
        for h in range(32):
            spread[:, 4096 * part_of + 128 * h : 4096 * part_of + 128 * h + 128] = put[4 * h : 4 * h + 3]

    finish_all(rig_copies)
    for j in range(9):
        if j == 4:
            continue

        @pl.when(exists(j // 3, j % 3))
        def _():
            slot_copy(j).wait_send()

    finish_all(copies)
    finish_all(wet_copies)
    dom_all.wait_send()
    slab_all.wait_send()


def on_device(doms, slabs, heat, emitting, shift, bucket, factor, rigidity, position, tally, accepting):
    dma = pltpu.SemaphoreType.DMA
    vm = pltpu.VMEM
    halos_out = [vm((2, 5, 8, 512), F32), vm((2, 2, 2, 8, 512), F32)]
    halos_in = [vm((2, 5, 8, 512), F32), vm((2, 5, 8, 512), F32), vm((2, 2, 2, 8, 512), F32)]
    halos = [halos_out[0], halos_in[0], halos_in[1], halos_out[1], halos_in[2]]
    whole = pl.BlockSpec(memory_space=pltpu.VMEM)
    away = pl.BlockSpec(memory_space=pl.ANY)
    return pl.pallas_call(
        functools.partial(kernel, doms, slabs),
        out_shape=[
            jax.ShapeDtypeStruct((3, 8, 8, 512), F32),
            jax.ShapeDtypeStruct((3, 16384), F32),
        ],
        in_specs=[whole, whole, away, away, away, whole, whole, whole, whole],
        out_specs=[whole, whole],
        scratch_shapes=[
            vm((4, 8, 8, 512), jnp.int32),
            vm((4, 8, 8, 512), jnp.int32),
            vm((4, 8, 8, 512), F32),
            vm((128, 256), BF16),
            vm((9, 64, 128), F32),
            vm((9, 64, 128), F32),
            vm((576, 256), BF16),
            vm((8, 8, 512), F32),
            *halos,
            *halos,
            vm((18, 16, 512), F32),
            vm((18, 16, 512), F32),
            *[vm((3, 16, 16, 512), F32) for _ in range(4)],
            vm((4, 3, 8, 8, 512), F32),
            vm((doms, 8, 128), F32),
            vm((slabs, 8, 128), F32),
            vm((3072, 256), BF16),
            vm((9, 16, 128), F32),
            vm((9, 16, 128), F32),
            dma((3,)),
            dma((9,)),
            dma((9,)),
            dma((9,)),
            dma((9,)),
            dma((9,)),
            dma((9,)),
            dma((9,)),
            dma((9,)),
            dma,
            dma,
            dma,
            dma,
        ],
        compiler_params=pltpu.CompilerParams(
            collective_id=0, has_side_effects=True, vmem_limit_bytes=56 * 2**20
        ),
    )(
        heat.reshape(128, 128),
        emitting.reshape(576, 128),
        shift,
        bucket,
        factor,
        rigidity,
        position.reshape(9, 1, 128),
        tally,
        accepting.reshape(9, 1, 128),
    )


def solution(mesh):
    in_specs = (
        P(BOTH),
        P(BOTH, None, None, None),
        P(None, DOM, SLAB, None),
        P(None, DOM, SLAB, None),
        P(None, DOM, SLAB, None),
        P(DOM, SLAB, None),
        P(BOTH, None, None, None),
        P(BOTH, None),
        P(BOTH, None, None, None),
    )
    out_specs = (P(None, DOM, SLAB, None), P(None, BOTH))
    return jax.shard_map(
        functools.partial(on_device, mesh.shape[DOM], mesh.shape[SLAB]),
        mesh=mesh,
        in_specs=in_specs,
        out_specs=out_specs,
        check_vma=False,
    )
```

```python
import functools

import jax
import jax.numpy as jnp
from jax import lax
from jax.experimental import pallas as pl
from jax.experimental.pallas import tpu as pltpu
from jax.sharding import PartitionSpec as P

DOM = "dom"
SLAB = "slab"
BOTH = ("dom", "slab")
MESH = pl.DeviceIdType.MESH
ITERS = 4
COEF = 0.5
CENTRE = 7.125
SPREAD = 6.875
F32 = jnp.float32
BF16 = jnp.bfloat16


def two_pieces(table):
    high = table.astype(BF16)
    low = (table - high.astype(F32)).astype(BF16)
    return high, low


def one_hot(across):
    width = across.shape[1]
    hot = lax.broadcasted_iota(jnp.int32, (256, width), 0) == across
    return jnp.where(hot, 1.0, 0.0).astype(BF16)


def pick_group(picked, groups, group):
    width = group.shape[1]
    picked = picked[:groups] + picked[groups:]
    apart = group - lax.broadcasted_iota(jnp.int32, (8, width), 0)
    total = jnp.zeros((8, width), F32)
    for k in range(groups // 8):
        total = jnp.where(apart == 8 * k, picked[8 * k : 8 * k + 8], total)
    return total


def look_up(pieces_ref, groups, across, group):
    picked = jnp.dot(pieces_ref[...], one_hot(across), preferred_element_type=F32)
    return pick_group(picked, groups, group)


def coefficients(moments):
    m = list(moments[:7])
    m[2], m[3] = 2.0 * m[2] - m[0], 2.0 * m[3] - m[1]
    m[4], m[5], m[6] = 2.0 * m[4] - m[0], 2.0 * m[5] - m[1], 2.0 * m[6] - m[0]
    gram = [[0.5 * (m[i + j] + m[abs(i - j)]) for j in range(4)] for i in range(4)]
    h = [[None] * 4 for _ in range(4)]
    for i in range(4):
        h[i][0] = gram[i][1]
        h[i][1] = 0.5 * (gram[i][0] + gram[i][2])
        h[i][2] = 0.5 * (gram[i][1] + gram[i][3])
    for i in range(3):
        h[i][3] = h[3][i]
    h[3][3] = moments[7]
    image = [[CENTRE * gram[i][j] + SPREAD * h[i][j] for j in range(4)] for i in range(4)]

    def form(matrix, v):
        n = len(v)
        return sum(
            (matrix[i][j] if i == j else 2.0 * matrix[i][j]) * v[i] * v[j]
            for i in range(n)
            for j in range(i, n)
        )

    one = jnp.ones_like(m[0])
    zero = jnp.zeros_like(m[0])
    x, r, p = [], [one], [one]
    rr = form(gram, r)
    for step in range(ITERS):
        alpha = rr / form(image, p)
        x = [(x[i] if i < len(x) else zero) + alpha * p[i] for i in range(len(p))]
        if step + 1 == ITERS:
            break
        shifted = [zero] * (len(p) + 1)
        for i, v in enumerate(p):
            shifted[i] = shifted[i] + CENTRE * v
            if i == 0:
                shifted[1] = shifted[1] + SPREAD * v
            else:
                shifted[i - 1] = shifted[i - 1] + 0.5 * SPREAD * v
                shifted[i + 1] = shifted[i + 1] + 0.5 * SPREAD * v
        r = [(r[i] if i < len(r) else zero) - alpha * shifted[i] for i in range(len(shifted))]
        new = form(gram, r)
        beta = new / rr
        p = [r[i] + beta * (p[i] if i < len(p) else zero) for i in range(len(r))]
        rr = new
    return x


def gather_tree(table_rows, across, group):
    found = [
        jnp.take_along_axis(jnp.broadcast_to(one, (8, 128)), across, axis=1, mode="promise_in_bounds")
        for one in table_rows
    ]
    bit = 0
    while len(found) > 1:
        odd = ((group >> bit) & 1) == 1
        found = [jnp.where(odd, found[k + 1], found[k]) for k in range(0, len(found), 2)]
        bit += 1
    return found[0]


def half_turn(tile):
    return pltpu.roll(tile, 4, 0)


def low_half(tile):
    return lax.broadcasted_iota(jnp.int32, tile.shape, 0) < 4


def pack_pair(near, far):
    return (
        jnp.where(low_half(near), near, half_turn(far)),
        jnp.where(low_half(near), half_turn(near), far),
    )


def pack_halos(block, side, corner):
    for x in range(4):
        side[0, x], side[1, x] = pack_pair(block[x], block[x + 4])
    for a in range(2):
        for j in range(2):
            corner[a, 0, j], corner[a, 1, j] = pack_pair(block[4 * a + j], block[4 * a + 2 + j])


def unpack_halos(block, side, dom, corner, wide):
    def put(at, middle, left, right):
        turned = half_turn(middle)
        wide[at, 0:8] = jnp.where(low_half(turned), left, turned)
        wide[at, 8:16] = jnp.where(low_half(turned), turned, right)

    for x in range(8):
        left, right = side[0, x % 4], side[1, x % 4]
        if x < 4:
            right = half_turn(right)
        else:
            left = half_turn(left)
        put(5 + x, block[x], left, right)
    for a in range(2):
        for t in range(5):
            u = t - 1 if a == 0 else t
            if 0 <= u < 4:
                left, right = corner[a, 0, u % 2], corner[a, 1, u % 2]
                if u < 2:
                    right = half_turn(right)
                else:
                    left = half_turn(left)
            else:
                left = right = jnp.zeros((8, 512), F32)
            put(t if a == 0 else 13 + t, dom[a, t], left, right)


def kernel(
    doms,
    slabs,
    heat,
    emitting,
    shift_hbm,
    bucket_hbm,
    factor_hbm,
    rigidity,
    wet_position,
    wet_tally,
    accepting,
    disp,
    spread,
    shift,
    bucket,
    factor,
    heat_pieces,
    slots_out,
    slots_in,
    pieces,
    interp,
    side_out,
    side_in,
    dom_in,
    corner_out,
    corner_in,
    rig_side_out,
    rig_side_in,
    rig_dom_in,
    rig_corner_out,
    rig_corner_in,
    wide,
    rig_wide,
    basis_0,
    basis_1,
    basis_2,
    basis_3,
    centre,
    dom_moments,
    slab_moments,
    wet_pieces,
    wet_out,
    wet_in,
    load_sem,
    slot_send,
    slot_recv,
    halo_send,
    halo_recv,
    rig_send,
    rig_recv,
    wet_send,
    wet_recv,
    dom_send,
    dom_recv,
    slab_send,
    slab_recv,
):
    d, s = lax.axis_index(DOM), lax.axis_index(SLAB)

    def exists(a, b):
        return (d + a >= 1) & (d + a <= doms) & (s + b >= 1) & (s + b <= slabs)

    loads = [
        pltpu.make_async_copy(src, dst, load_sem.at[i])
        for i, (src, dst) in enumerate(((shift_hbm, shift), (bucket_hbm, bucket), (factor_hbm, factor)))
    ]
    for load in loads:
        load.start()

    barrier = pltpu.get_barrier_semaphore()
    for k in range(1, doms):
        pl.semaphore_signal(barrier, inc=1, device_id=(lax.rem(d + k, doms), s), device_id_type=MESH)
    for k in range(1, slabs):
        pl.semaphore_signal(barrier, inc=1, device_id=(d, lax.rem(s + k, slabs)), device_id_type=MESH)
    expected = doms + slabs - 2
    for a in (0, 2):
        for b in (0, 2):

            @pl.when(exists(a, b))
            def _():
                pl.semaphore_signal(
                    barrier, inc=1, device_id=(d + (a - 1), s + (b - 1)), device_id_type=MESH
                )

            expected = expected + exists(a, b).astype(jnp.int32)

    def halo_copies(block, s_out, s_in, d_in, c_out, c_in, send, recv):
        found = []
        for a in range(3):
            for b in range(3):
                if a == 1 and b == 1:
                    continue
                if a == 1:
                    src, dst = s_out.at[b // 2], s_in.at[1 - b // 2]
                elif b == 1:
                    src, dst = block.at[pl.ds(3 if a == 2 else 0, 5)], d_in.at[1 - a // 2]
                else:
                    src, dst = c_out.at[a // 2, b // 2], c_in.at[1 - a // 2, 1 - b // 2]
                j = 3 * a + b
                copy = pltpu.make_async_remote_copy(
                    src_ref=src,
                    dst_ref=dst,
                    send_sem=send.at[j],
                    recv_sem=recv.at[8 - j],
                    device_id=(d + (a - 1), s + (b - 1)),
                    device_id_type=MESH,
                )
                found.append((a, b, copy))
        return found

    def start_all(copies):
        for a, b, copy in copies:

            @pl.when(exists(a, b))
            def _():
                copy.start()

    def receive_all(copies):
        for a, b, copy in copies:

            @pl.when(exists(2 - a, 2 - b))
            def _():
                copy.wait_recv()

    def finish_all(copies):
        for a, b, copy in copies:

            @pl.when(exists(a, b))
            def _():
                copy.wait_send()

    def clear_missing(s_in, d_in, c_in):
        for a in range(3):
            for b in range(3):
                if a == 1 and b == 1:
                    continue

                @pl.when(jnp.logical_not(exists(a, b)))
                def _():
                    if a == 1:
                        s_in[b // 2] = jnp.zeros((5, 8, 512), F32)
                    elif b == 1:
                        d_in[a // 2] = jnp.zeros((5, 8, 512), F32)
                    else:
                        c_in[a // 2, b // 2] = jnp.zeros((2, 8, 512), F32)

    def clear_blocks(blocks):
        for j in range(9):
            if j == 4:
                continue

            @pl.when(jnp.logical_not(exists(j // 3, j % 3)))
            def _():
                blocks[j] = jnp.zeros(blocks.shape[1:], F32)

    heat_pieces[:64], heat_pieces[64:] = two_pieces(jnp.concatenate([heat[:64], heat[64:]], axis=1))
    clear_missing(rig_side_in, rig_dom_in, rig_corner_in)
    clear_missing(side_in, dom_in, corner_in)
    clear_blocks(slots_in)
    clear_blocks(wet_in)
    wet_out[...] = jnp.zeros(wet_out.shape, F32)
    rig_copies = halo_copies(
        rigidity, rig_side_out, rig_side_in, rig_dom_in, rig_corner_out, rig_corner_in, rig_send, rig_recv
    )
    def slot_copy(j):
        return pltpu.make_async_remote_copy(
            src_ref=slots_out.at[j],
            dst_ref=slots_in.at[8 - j],
            send_sem=slot_send.at[j],
            recv_sem=slot_recv.at[8 - j],
            device_id=(d + (j // 3 - 1), s + (j % 3 - 1)),
            device_id_type=MESH,
        )

    def start_slot(j):
        @pl.when((j != 4) & exists(j // 3, lax.rem(j, 3)))
        def _():
            slot_copy(j).start()

    def slot_block(t, carry):
        j = lax.rem(t + 5, 9)
        for i in range(16):
            k = jnp.concatenate([emitting[pl.ds(64 * j + 2 * i + r, 1), :] for r in range(2)], axis=1)
            across = (k >> 13) * 128 + (k & 127)
            found = look_up(heat_pieces, 64, across, (k >> 7) & 63)
            found = jnp.sum(found, axis=0, keepdims=True)
            slots_out[j, 2 * i : 2 * i + 1] = found[:, :128]
            slots_out[j, 2 * i + 1 : 2 * i + 2] = found[:, 128:]
        for i in range(4, 8):
            k = emitting[pl.ds(pl.multiple_of(64 * j + 8 * i, 8), 8), :]
            slots_out[j, 8 * i : 8 * i + 8] = gather_tree([heat[r : r + 1] for r in range(128)], k & 127, k >> 7)

        @pl.when(t == 3)
        def _():
            pl.semaphore_wait(barrier, expected)
            for early in (5, 6, 7):
                start_slot(jnp.int32(early))

        @pl.when(t >= 3)
        def _():
            start_slot(j)

        return carry

    lax.fori_loop(0, 9, slot_block, 0)
    pack_halos(rigidity, rig_side_out, rig_corner_out)
    for b in range(2):
        rig_side_out[b, 4] = jnp.zeros((8, 512), F32)
    start_all(rig_copies)
    slots_in[4] = slots_out[4]
    for load in loads:
        load.wait()
    for j in range(9):
        if j == 4:
            continue

        @pl.when(exists(2 - j // 3, 2 - j % 3))
        def _():
            slot_copy(j).wait_recv()

    for h in range(9):
        table = jnp.concatenate([slots_in[h, :32], slots_in[h, 32:]], axis=1)
        pieces[32 * h : 32 * h + 32], pieces[288 + 32 * h : 320 + 32 * h] = two_pieces(table)

    def matched(k, holder):
        return look_up(pieces, 288, ((k >> 12) & 1) * 128 + (k & 127), holder * 32 + ((k >> 7) & 31))

    def plane(x, carry):
        def rows(half_plane, last):
            for u in range(2):
                q = 2 * half_plane + u

                def pair(ref, corner):
                    ends = [ref[corner, x, pl.ds(2 * q + i, 1), pl.ds(256, 256)] for i in range(2)]
                    return jnp.concatenate([end[:, :128] for end in ends], axis=1)

                for i in range(2):
                    total = jnp.zeros((8, 256), F32)
                    for corner in range(4):
                        at = (corner, x, pl.ds(2 * q + i, 1), pl.ds(0, 256))
                        total = total + matched(bucket[at], shift[at]) * factor[at]
                    interp[x, pl.ds(2 * q + i, 1), pl.ds(0, 256)] = jnp.sum(total, axis=0, keepdims=True)
                total = jnp.zeros((8, 256), F32)
                for corner in range(4):
                    total = total + matched(pair(bucket, corner), pair(shift, corner)) * pair(factor, corner)
                total = jnp.sum(total, axis=0, keepdims=True)
                for i in range(2):
                    both = jnp.concatenate([total[:, 128 * i : 128 * i + 128]] * 2, axis=1)
                    interp[x, pl.ds(2 * q + i, 1), pl.ds(256, 256)] = both

                at = (q, x, slice(None), pl.ds(384, 128))
                k, holder = bucket[at], shift[at]
                found = None
                for h in range(9):
                    one = gather_tree([slots_in[h, r : r + 1] for r in range(64)], k & 127, k >> 7)
                    found = one if found is None else jnp.where(holder == h, one, found)
                last = last + factor[at] * found
            return last

        interp[x, :, 384:512] = lax.fori_loop(0, 2, rows, jnp.zeros((8, 128), F32))
        return carry

    copies = halo_copies(interp, side_out, side_in, dom_in, corner_out, corner_in, halo_send, halo_recv)

    def send_piece(a, b, src, dst):
        j = 3 * a + b

        @pl.when(exists(a, b))
        def _():
            pltpu.make_async_remote_copy(
                src_ref=src,
                dst_ref=dst,
                send_sem=halo_send.at[j],
                recv_sem=halo_recv.at[8 - j],
                device_id=(d + (a - 1), s + (b - 1)),
                device_id_type=MESH,
            ).start()

    def plane_pair(q, carry):
        p = lax.rem(2 * q, 4) + q // 2
        lax.fori_loop(0, 2, lambda e, carry: plane(p + 4 * e, carry), 0)
        near, far = interp[p], interp[p + 4]
        side_out[0, p], side_out[1, p] = pack_pair(near, far)
        for b in range(2):
            side_out[b, 4, pl.ds(p, 1), :] = near[4 - b : 5 - b]
            side_out[b, 4, pl.ds(p + 4, 1), :] = far[4 - b : 5 - b]
            send_piece(1, 2 * b, side_out.at[b, p], side_in.at[1 - b, p])
        send_piece(0, 1, interp.at[p], dom_in.at[1, p])
        send_piece(2, 1, interp.at[p + 4], dom_in.at[0, p + 1])

        @pl.when(q == 0)
        def _():
            send_piece(0, 1, interp.at[4], dom_in.at[1, 4])

        @pl.when(q % 2 == 1)
        def _():
            j = q // 2
            for a in range(2):
                pieces_of = pack_pair(interp[4 * a + j], interp[4 * a + 2 + j])
                for b in range(2):
                    corner_out[a, b, j] = pieces_of[b]
                    send_piece(2 * a, 2 * b, corner_out.at[a, b, j], corner_in.at[1 - a, 1 - b, j])

        @pl.when(q == 3)
        def _():
            send_piece(2, 1, interp.at[3], dom_in.at[0, 0])
            for b in range(2):
                send_piece(1, 2 * b, side_out.at[b, 4], side_in.at[1 - b, 4])

        return carry

    lax.fori_loop(0, 4, plane_pair, 0)

    receive_all(rig_copies)
    unpack_halos(rigidity, rig_side_in, rig_dom_in, rig_corner_in, rig_wide)
    receive_all(copies)
    unpack_halos(interp, side_in, dom_in, corner_in, wide)

    row = lax.broadcasted_iota(jnp.int32, (16, 512), 0)
    lane = lax.broadcasted_iota(jnp.int32, (16, 512), 1)
    row_inside = ((row >= 4) | (s > 0)) & ((row < 12) | (s < slabs - 1))

    def inside(xx):
        return row_inside & ((xx >= 4) | (d > 0)) & ((xx < 12) | (d < doms - 1))

    def back_z(v):
        return jnp.where(lane == 0, 0.0, pltpu.roll(v, 1, 1))

    def ahead_z(v):
        return jnp.where(lane == 511, 0.0, pltpu.roll(v, 511, 1))

    basis = (basis_0, basis_1, basis_2, basis_3)

    def in_groups(first, end, size, body, carry):
        def group(i, carry):
            for k in range(size):
                carry = body(first + size * i + k, carry)
            return carry

        return lax.fori_loop(0, (end - first) // size, group, carry)

    def load_plane(xx, carry):
        here = wide[xx + 1]
        keep = inside(xx)
        at = jnp.clip(xx - 4, 0, 7)
        back = jnp.where(row == 0, side_in[0, 4, pl.ds(at, 1), :], pltpu.roll(here, 1, 0))
        ahead = jnp.where(row == 15, side_in[1, 4, pl.ds(at, 1), :], pltpu.roll(here, 15, 0))
        basis_0[0, xx] = jnp.where(keep, COEF * (wide[xx + 2] - wide[xx]), 0.0)
        basis_0[1, xx] = jnp.where(keep, COEF * (ahead - back), 0.0)
        basis_0[2, xx] = jnp.where(keep, COEF * (ahead_z(here) - back_z(here)), 0.0)
        return carry

    in_groups(0, 16, 4, load_plane, 0)

    def scaled_operate(level, c, xx):
        v = basis[level][c, xx]
        beside = basis[level][c, xx - 1] + basis[level][c, xx + 1]
        beside = beside + pltpu.roll(v, 1, 0) + pltpu.roll(v, 15, 0)
        beside = beside + back_z(v) + ahead_z(v)
        return ((rig_wide[xx + 1] + (6.0 - CENTRE)) * v - beside) * (1.0 / SPREAD)

    for level in range(1, 4):

        def next_plane(xx, carry, level=level):
            keep = inside(xx)
            for c in range(3):
                image = scaled_operate(level - 1, c, xx)
                if level > 1:
                    image = 2.0 * image - basis[level - 2][c, xx]
                basis[level][c, xx] = jnp.where(keep, image, 0.0)
            return carry

        in_groups(level, 16 - level, (7, 4, 5)[level - 1], next_plane, 0)

    def folded(field):
        return jnp.where(low_half(field[:8]), field[8:], field[:8])

    def moment_plane(xx, totals):
        totals = list(totals)
        for c in range(3):
            w = [folded(basis[level][c, xx]) for level in range(4)]
            for level in range(4):
                centre[level, c, xx - 4] = w[level]
            w.append(folded(scaled_operate(3, c, xx)))
            pairs = ((0, 0), (0, 1), (1, 1), (1, 2), (2, 2), (2, 3), (3, 3), (3, 4))
            for i, (one, two) in enumerate(pairs):
                product = w[one] * w[two]
                product = (product[:, :128] + product[:, 128:256]) + (product[:, 256:384] + product[:, 384:])
                totals[i] = totals[i] + product
        return tuple(totals)

    totals = in_groups(4, 12, 4, moment_plane, tuple(jnp.zeros((8, 128), F32) for _ in range(8)))
    for i in range(8):
        dom_moments[0, i : i + 1] = jnp.sum(totals[i], axis=0, keepdims=True)

    def reduce_copy(buffer, send, recv, source, target, device):
        return pltpu.make_async_remote_copy(
            src_ref=buffer.at[source],
            dst_ref=buffer.at[target],
            send_sem=send,
            recv_sem=recv,
            device_id=device,
            device_id_type=MESH,
        )

    for k in range(1, doms):
        reduce_copy(dom_moments, dom_send, dom_recv, 0, k, (lax.rem(d + k, doms), s)).start()
    others = pl.ds(1, doms - 1)
    dom_all = reduce_copy(dom_moments, dom_send, dom_recv, others, others, (lax.rem(d + 1, doms), s))
    others = pl.ds(1, slabs - 1)
    slab_all = reduce_copy(slab_moments, slab_send, slab_recv, others, others, (d, lax.rem(s + 1, slabs)))

    for level in range(4):
        for c in range(3):
            for x in range(8):
                for half in range(2):
                    high, low = two_pieces(centre[level, c, x, :, 256 * half : 256 * half + 256])
                    at = 16 * x + 8 * half
                    at = at + 256 * (3 * level + c)
                    wet_pieces[at : at + 8] = high
                    wet_pieces[128 + at : 136 + at] = low

    def wet_block(a):
        node = jnp.concatenate([wet_position[3 * a + b] for b in range(3)], axis=1)
        group = (node >> 12) * 16 + ((node >> 8) & 1) * 8 + (((node >> 9) + 4) & 7)
        slot = lax.broadcasted_iota(jnp.int32, (1, 128), 1)
        live = jnp.concatenate(
            [slot < wet_tally[0:1, 3 * a + b : 3 * a + b + 1] for b in range(3)], axis=1
        )
        picked = jnp.dot(wet_pieces[...], one_hot(node & 255), preferred_element_type=F32)
        for kc in range(12):
            found = pick_group(picked[256 * kc : 256 * kc + 256], 128, group)
            found = jnp.where(live, jnp.sum(found, axis=0, keepdims=True), 0.0)
            at = kc // 3 * 4 + kc % 3
            for b in range(3):
                wet_out[3 * a + b, at : at + 1] = found[:, 128 * b : 128 * b + 128]

    wet_block(0)
    dom_all.wait_recv()
    total = dom_moments[0]
    for k in range(1, doms):
        total = total + dom_moments[k]
    slab_moments[0] = total
    for k in range(1, slabs):
        reduce_copy(slab_moments, slab_send, slab_recv, 0, k, (d, lax.rem(s + k, slabs))).start()
    wet_block(1)
    wet_block(2)

    wet_copies = []
    for j in range(9):
        if j == 4:
            continue
        copy = pltpu.make_async_remote_copy(
            src_ref=wet_out.at[j],
            dst_ref=wet_in.at[8 - j],
            send_sem=wet_send.at[j],
            recv_sem=wet_recv.at[8 - j],
            device_id=(d + (j // 3 - 1), s + (j % 3 - 1)),
            device_id_type=MESH,
        )
        wet_copies.append((j // 3, j % 3, copy))
    start_all(wet_copies)
    wet_in[4] = wet_out[4]

    taker = jnp.concatenate([accepting[j] for j in range(9)], axis=1)
    lane_of = lax.broadcasted_iota(jnp.int32, (128, 1152), 0)
    lane_hot = jnp.where(lane_of == (taker & 127), 1.0, 0.0).astype(BF16)

    slab_all.wait_recv()
    total = slab_moments[0]
    for k in range(1, slabs):
        total = total + slab_moments[k]
    c = coefficients([jnp.sum(total[i : i + 1], axis=1, keepdims=True) for i in range(8)])

    def combine(x, carry):
        for a in range(3):
            field = c[0] * centre[0, a, x]
            for level in range(1, 4):
                field = field + c[level] * centre[level, a, x]
            disp[a, x] = half_turn(field)
        return carry

    lax.fori_loop(0, 8, combine, 0)

    receive_all(wet_copies)
    sub = lax.broadcasted_iota(jnp.int32, (8, 1), 0)
    first = jnp.where(sub < 4, c[0], c[1])
    second = jnp.where(sub < 4, c[2], c[3])
    value = jnp.concatenate([wet_in[j, :8] * first + wet_in[j, 8:] * second for j in range(9)], axis=1)
    value = value + half_turn(value)
    high = value.astype(BF16).astype(F32)
    apart = (taker >> 7) - (lax.broadcasted_iota(jnp.int32, (8, 1152), 0) >> 2)
    for part_of in range(4):
        at = range(16 * part_of, 16 * part_of + 16)
        lines = [
            jnp.where(apart == 2 * h, part, 0.0).astype(BF16) for part in (high, value - high) for h in at
        ]
        put = lax.dot_general(
            jnp.concatenate(lines, axis=0), lane_hot, (((1,), (1,)), ((), ())), preferred_element_type=F32
        )
        put = put[:128] + put[128:]
        for h in range(32):
            spread[:, 4096 * part_of + 128 * h : 4096 * part_of + 128 * h + 128] = put[4 * h : 4 * h + 3]

    finish_all(rig_copies)
    for j in range(9):
        if j == 4:
            continue

        @pl.when(exists(j // 3, j % 3))
        def _():
            slot_copy(j).wait_send()

    finish_all(copies)
    finish_all(wet_copies)
    dom_all.wait_send()
    slab_all.wait_send()


def on_device(doms, slabs, heat, emitting, shift, bucket, factor, rigidity, position, tally, accepting):
    dma = pltpu.SemaphoreType.DMA
    vm = pltpu.VMEM
    halos_out = [vm((2, 5, 8, 512), F32), vm((2, 2, 2, 8, 512), F32)]
    halos_in = [vm((2, 5, 8, 512), F32), vm((2, 5, 8, 512), F32), vm((2, 2, 2, 8, 512), F32)]
    halos = [halos_out[0], halos_in[0], halos_in[1], halos_out[1], halos_in[2]]
    whole = pl.BlockSpec(memory_space=pltpu.VMEM)
    away = pl.BlockSpec(memory_space=pl.ANY)
    return pl.pallas_call(
        functools.partial(kernel, doms, slabs),
        out_shape=[
            jax.ShapeDtypeStruct((3, 8, 8, 512), F32),
            jax.ShapeDtypeStruct((3, 16384), F32),
        ],
        in_specs=[whole, whole, away, away, away, whole, whole, whole, whole],
        out_specs=[whole, whole],
        scratch_shapes=[
            vm((4, 8, 8, 512), jnp.int32),
            vm((4, 8, 8, 512), jnp.int32),
            vm((4, 8, 8, 512), F32),
            vm((128, 256), BF16),
            vm((9, 64, 128), F32),
            vm((9, 64, 128), F32),
            vm((576, 256), BF16),
            vm((8, 8, 512), F32),
            *halos,
            *halos,
            vm((18, 16, 512), F32),
            vm((18, 16, 512), F32),
            *[vm((3, 16, 16, 512), F32) for _ in range(4)],
            vm((4, 3, 8, 8, 512), F32),
            vm((doms, 8, 128), F32),
            vm((slabs, 8, 128), F32),
            vm((3072, 256), BF16),
            vm((9, 16, 128), F32),
            vm((9, 16, 128), F32),
            dma((3,)),
            dma((9,)),
            dma((9,)),
            dma((9,)),
            dma((9,)),
            dma((9,)),
            dma((9,)),
            dma((9,)),
            dma((9,)),
            dma,
            dma,
            dma,
            dma,
        ],
        compiler_params=pltpu.CompilerParams(
            collective_id=0, has_side_effects=True, vmem_limit_bytes=56 * 2**20
        ),
    )(
        heat.reshape(128, 128),
        emitting.reshape(576, 128),
        shift,
        bucket,
        factor,
        rigidity,
        position.reshape(9, 1, 128),
        tally,
        accepting.reshape(9, 1, 128),
    )


def solution(mesh):
    in_specs = (
        P(BOTH),
        P(BOTH, None, None, None),
        P(None, DOM, SLAB, None),
        P(None, DOM, SLAB, None),
        P(None, DOM, SLAB, None),
        P(DOM, SLAB, None),
        P(BOTH, None, None, None),
        P(BOTH, None),
        P(BOTH, None, None, None),
    )
    out_specs = (P(None, DOM, SLAB, None), P(None, BOTH))
    return jax.shard_map(
        functools.partial(on_device, mesh.shape[DOM], mesh.shape[SLAB]),
        mesh=mesh,
        in_specs=in_specs,
        out_specs=out_specs,
        check_vma=False,
    )
```

```python
import functools

import jax
import jax.numpy as jnp
from jax import lax
from jax.experimental import pallas as pl
from jax.experimental.pallas import tpu as pltpu
from jax.sharding import PartitionSpec as P

DOM = "dom"
SLAB = "slab"
BOTH = ("dom", "slab")
MESH = pl.DeviceIdType.MESH
ITERS = 4
COEF = 0.5
CENTRE = 7.125
SPREAD = 6.875
F32 = jnp.float32
BF16 = jnp.bfloat16


def two_pieces(table):
    high = table.astype(BF16)
    low = (table - high.astype(F32)).astype(BF16)
    return high, low


def one_hot(across):
    width = across.shape[1]
    hot = lax.broadcasted_iota(jnp.int32, (256, width), 0) == across
    return jnp.where(hot, 1.0, 0.0).astype(BF16)


def pick_group(picked, groups, group):
    width = group.shape[1]
    picked = picked[:groups] + picked[groups:]
    apart = group - lax.broadcasted_iota(jnp.int32, (8, width), 0)
    total = jnp.zeros((8, width), F32)
    for k in range(groups // 8):
        total = jnp.where(apart == 8 * k, picked[8 * k : 8 * k + 8], total)
    return total


def look_up(pieces_ref, groups, across, group):
    picked = jnp.dot(pieces_ref[...], one_hot(across), preferred_element_type=F32)
    return pick_group(picked, groups, group)


def coefficients(moments):
    m = list(moments[:7])
    m[2], m[3] = 2.0 * m[2] - m[0], 2.0 * m[3] - m[1]
    m[4], m[5], m[6] = 2.0 * m[4] - m[0], 2.0 * m[5] - m[1], 2.0 * m[6] - m[0]
    gram = [[0.5 * (m[i + j] + m[abs(i - j)]) for j in range(4)] for i in range(4)]
    h = [[None] * 4 for _ in range(4)]
    for i in range(4):
        h[i][0] = gram[i][1]
        h[i][1] = 0.5 * (gram[i][0] + gram[i][2])
        h[i][2] = 0.5 * (gram[i][1] + gram[i][3])
    for i in range(3):
        h[i][3] = h[3][i]
    h[3][3] = moments[7]
    image = [[CENTRE * gram[i][j] + SPREAD * h[i][j] for j in range(4)] for i in range(4)]

    def form(matrix, v):
        n = len(v)
        return sum(
            (matrix[i][j] if i == j else 2.0 * matrix[i][j]) * v[i] * v[j]
            for i in range(n)
            for j in range(i, n)
        )

    one = jnp.ones_like(m[0])
    zero = jnp.zeros_like(m[0])
    x, r, p = [], [one], [one]
    rr = form(gram, r)
    for step in range(ITERS):
        alpha = rr / form(image, p)
        x = [(x[i] if i < len(x) else zero) + alpha * p[i] for i in range(len(p))]
        if step + 1 == ITERS:
            break
        shifted = [zero] * (len(p) + 1)
        for i, v in enumerate(p):
            shifted[i] = shifted[i] + CENTRE * v
            if i == 0:
                shifted[1] = shifted[1] + SPREAD * v
            else:
                shifted[i - 1] = shifted[i - 1] + 0.5 * SPREAD * v
                shifted[i + 1] = shifted[i + 1] + 0.5 * SPREAD * v
        r = [(r[i] if i < len(r) else zero) - alpha * shifted[i] for i in range(len(shifted))]
        new = form(gram, r)
        beta = new / rr
        p = [r[i] + beta * (p[i] if i < len(p) else zero) for i in range(len(r))]
        rr = new
    return x


def gather_tree(table_rows, across, group):
    found = [
        jnp.take_along_axis(jnp.broadcast_to(one, (8, 128)), across, axis=1, mode="promise_in_bounds")
        for one in table_rows
    ]
    bit = 0
    while len(found) > 1:
        odd = ((group >> bit) & 1) == 1
        found = [jnp.where(odd, found[k + 1], found[k]) for k in range(0, len(found), 2)]
        bit += 1
    return found[0]


def half_turn(tile):
    return pltpu.roll(tile, 4, 0)


def low_half(tile):
    return lax.broadcasted_iota(jnp.int32, tile.shape, 0) < 4


def pack_pair(near, far):
    return (
        jnp.where(low_half(near), near, half_turn(far)),
        jnp.where(low_half(near), half_turn(near), far),
    )


def pack_halos(block, side, corner):
    for x in range(4):
        side[0, x], side[1, x] = pack_pair(block[x], block[x + 4])
    for a in range(2):
        for j in range(2):
            corner[a, 0, j], corner[a, 1, j] = pack_pair(block[4 * a + j], block[4 * a + 2 + j])


def unpack_halos(block, side, dom, corner, wide):
    def put(at, middle, left, right):
        turned = half_turn(middle)
        wide[at, 0:8] = jnp.where(low_half(turned), left, turned)
        wide[at, 8:16] = jnp.where(low_half(turned), turned, right)

    for x in range(8):
        left, right = side[0, x % 4], side[1, x % 4]
        if x < 4:
            right = half_turn(right)
        else:
            left = half_turn(left)
        put(5 + x, block[x], left, right)
    for a in range(2):
        for t in range(5):
            u = t - 1 if a == 0 else t
            if 0 <= u < 4:
                left, right = corner[a, 0, u % 2], corner[a, 1, u % 2]
                if u < 2:
                    right = half_turn(right)
                else:
                    left = half_turn(left)
            else:
                left = right = jnp.zeros((8, 512), F32)
            put(t if a == 0 else 13 + t, dom[a, t], left, right)


def kernel(
    doms,
    slabs,
    heat,
    emitting,
    shift_hbm,
    bucket_hbm,
    factor_hbm,
    rigidity,
    wet_position,
    wet_tally,
    accepting,
    disp,
    spread,
    shift,
    bucket,
    factor,
    heat_pieces,
    slots_out,
    slots_in,
    pieces,
    interp,
    side_out,
    side_in,
    dom_in,
    corner_out,
    corner_in,
    rig_side_out,
    rig_side_in,
    rig_dom_in,
    rig_corner_out,
    rig_corner_in,
    wide,
    rig_wide,
    basis_0,
    basis_1,
    basis_2,
    basis_3,
    centre,
    dom_moments,
    slab_moments,
    wet_pieces,
    wet_out,
    wet_in,
    load_sem,
    slot_send,
    slot_recv,
    halo_send,
    halo_recv,
    rig_send,
    rig_recv,
    wet_send,
    wet_recv,
    dom_send,
    dom_recv,
    slab_send,
    slab_recv,
):
    d, s = lax.axis_index(DOM), lax.axis_index(SLAB)

    def exists(a, b):
        return (d + a >= 1) & (d + a <= doms) & (s + b >= 1) & (s + b <= slabs)

    loads = [
        pltpu.make_async_copy(src, dst, load_sem.at[i])
        for i, (src, dst) in enumerate(((shift_hbm, shift), (bucket_hbm, bucket), (factor_hbm, factor)))
    ]
    for load in loads:
        load.start()

    barrier = pltpu.get_barrier_semaphore()
    for k in range(1, doms):
        pl.semaphore_signal(barrier, inc=1, device_id=(lax.rem(d + k, doms), s), device_id_type=MESH)
    for k in range(1, slabs):
        pl.semaphore_signal(barrier, inc=1, device_id=(d, lax.rem(s + k, slabs)), device_id_type=MESH)
    expected = doms + slabs - 2
    for a in (0, 2):
        for b in (0, 2):

            @pl.when(exists(a, b))
            def _():
                pl.semaphore_signal(
                    barrier, inc=1, device_id=(d + (a - 1), s + (b - 1)), device_id_type=MESH
                )

            expected = expected + exists(a, b).astype(jnp.int32)

    def halo_copies(block, s_out, s_in, d_in, c_out, c_in, send, recv):
        found = []
        for a in range(3):
            for b in range(3):
                if a == 1 and b == 1:
                    continue
                if a == 1:
                    src, dst = s_out.at[b // 2], s_in.at[1 - b // 2]
                elif b == 1:
                    src, dst = block.at[pl.ds(3 if a == 2 else 0, 5)], d_in.at[1 - a // 2]
                else:
                    src, dst = c_out.at[a // 2, b // 2], c_in.at[1 - a // 2, 1 - b // 2]
                j = 3 * a + b
                copy = pltpu.make_async_remote_copy(
                    src_ref=src,
                    dst_ref=dst,
                    send_sem=send.at[j],
                    recv_sem=recv.at[8 - j],
                    device_id=(d + (a - 1), s + (b - 1)),
                    device_id_type=MESH,
                )
                found.append((a, b, copy))
        return found

    def start_all(copies):
        for a, b, copy in copies:

            @pl.when(exists(a, b))
            def _():
                copy.start()

    def receive_all(copies):
        for a, b, copy in copies:

            @pl.when(exists(2 - a, 2 - b))
            def _():
                copy.wait_recv()

    def finish_all(copies):
        for a, b, copy in copies:

            @pl.when(exists(a, b))
            def _():
                copy.wait_send()

    def clear_missing(s_in, d_in, c_in):
        for a in range(3):
            for b in range(3):
                if a == 1 and b == 1:
                    continue

                @pl.when(jnp.logical_not(exists(a, b)))
                def _():
                    if a == 1:
                        s_in[b // 2] = jnp.zeros((5, 8, 512), F32)
                    elif b == 1:
                        d_in[a // 2] = jnp.zeros((5, 8, 512), F32)
                    else:
                        c_in[a // 2, b // 2] = jnp.zeros((2, 8, 512), F32)

    def clear_blocks(blocks):
        for j in range(9):
            if j == 4:
                continue

            @pl.when(jnp.logical_not(exists(j // 3, j % 3)))
            def _():
                blocks[j] = jnp.zeros(blocks.shape[1:], F32)

    heat_pieces[:64], heat_pieces[64:] = two_pieces(jnp.concatenate([heat[:64], heat[64:]], axis=1))
    clear_missing(rig_side_in, rig_dom_in, rig_corner_in)
    clear_missing(side_in, dom_in, corner_in)
    clear_blocks(slots_in)
    clear_blocks(wet_in)
    wet_out[...] = jnp.zeros(wet_out.shape, F32)
    rig_copies = halo_copies(
        rigidity, rig_side_out, rig_side_in, rig_dom_in, rig_corner_out, rig_corner_in, rig_send, rig_recv
    )
    def slot_copy(j):
        return pltpu.make_async_remote_copy(
            src_ref=slots_out.at[j],
            dst_ref=slots_in.at[8 - j],
            send_sem=slot_send.at[j],
            recv_sem=slot_recv.at[8 - j],
            device_id=(d + (j // 3 - 1), s + (j % 3 - 1)),
            device_id_type=MESH,
        )

    def start_slot(j):
        @pl.when((j != 4) & exists(j // 3, lax.rem(j, 3)))
        def _():
            slot_copy(j).start()

    def slot_block(t, carry):
        j = lax.rem(t + 5, 9)
        for i in range(16):
            k = jnp.concatenate([emitting[pl.ds(64 * j + 2 * i + r, 1), :] for r in range(2)], axis=1)
            across = (k >> 13) * 128 + (k & 127)
            found = look_up(heat_pieces, 64, across, (k >> 7) & 63)
            found = jnp.sum(found, axis=0, keepdims=True)
            slots_out[j, 2 * i : 2 * i + 1] = found[:, :128]
            slots_out[j, 2 * i + 1 : 2 * i + 2] = found[:, 128:]
        for i in range(4, 8):
            k = emitting[pl.ds(pl.multiple_of(64 * j + 8 * i, 8), 8), :]
            slots_out[j, 8 * i : 8 * i + 8] = gather_tree([heat[r : r + 1] for r in range(128)], k & 127, k >> 7)

        @pl.when(t == 3)
        def _():
            pl.semaphore_wait(barrier, expected)
            for early in (5, 6, 7):
                start_slot(jnp.int32(early))

        @pl.when(t >= 3)
        def _():
            start_slot(j)

        return carry

    lax.fori_loop(0, 9, slot_block, 0)
    pack_halos(rigidity, rig_side_out, rig_corner_out)
    for b in range(2):
        rig_side_out[b, 4] = jnp.zeros((8, 512), F32)
    start_all(rig_copies)
    slots_in[4] = slots_out[4]
    for load in loads:
        load.wait()
    for j in range(9):
        if j == 4:
            continue

        @pl.when(exists(2 - j // 3, 2 - j % 3))
        def _():
            slot_copy(j).wait_recv()

    for h in range(9):
        table = jnp.concatenate([slots_in[h, :32], slots_in[h, 32:]], axis=1)
        pieces[32 * h : 32 * h + 32], pieces[288 + 32 * h : 320 + 32 * h] = two_pieces(table)

    def matched(k, holder):
        return look_up(pieces, 288, ((k >> 12) & 1) * 128 + (k & 127), holder * 32 + ((k >> 7) & 31))

    def plane(x, carry):
        def rows(half_plane, last):
            for u in range(2):
                q = 2 * half_plane + u

                def pair(ref, corner):
                    ends = [ref[corner, x, pl.ds(2 * q + i, 1), pl.ds(256, 256)] for i in range(2)]
                    return jnp.concatenate([end[:, :128] for end in ends], axis=1)

                for i in range(2):
                    total = jnp.zeros((8, 256), F32)
                    for corner in range(4):
                        at = (corner, x, pl.ds(2 * q + i, 1), pl.ds(0, 256))
                        total = total + matched(bucket[at], shift[at]) * factor[at]
                    interp[x, pl.ds(2 * q + i, 1), pl.ds(0, 256)] = jnp.sum(total, axis=0, keepdims=True)
                total = jnp.zeros((8, 256), F32)
                for corner in range(4):
                    total = total + matched(pair(bucket, corner), pair(shift, corner)) * pair(factor, corner)
                total = jnp.sum(total, axis=0, keepdims=True)
                for i in range(2):
                    both = jnp.concatenate([total[:, 128 * i : 128 * i + 128]] * 2, axis=1)
                    interp[x, pl.ds(2 * q + i, 1), pl.ds(256, 256)] = both

                at = (q, x, slice(None), pl.ds(384, 128))
                k, holder = bucket[at], shift[at]
                found = None
                for h in range(9):
                    one = gather_tree([slots_in[h, r : r + 1] for r in range(64)], k & 127, k >> 7)
                    found = one if found is None else jnp.where(holder == h, one, found)
                last = last + factor[at] * found
            return last

        interp[x, :, 384:512] = lax.fori_loop(0, 2, rows, jnp.zeros((8, 128), F32))
        return carry

    copies = halo_copies(interp, side_out, side_in, dom_in, corner_out, corner_in, halo_send, halo_recv)

    def send_piece(a, b, src, dst):
        j = 3 * a + b

        @pl.when(exists(a, b))
        def _():
            pltpu.make_async_remote_copy(
                src_ref=src,
                dst_ref=dst,
                send_sem=halo_send.at[j],
                recv_sem=halo_recv.at[8 - j],
                device_id=(d + (a - 1), s + (b - 1)),
                device_id_type=MESH,
            ).start()

    def plane_pair(q, carry):
        p = lax.rem(2 * q, 4) + q // 2
        lax.fori_loop(0, 2, lambda e, carry: plane(p + 4 * e, carry), 0)
        near, far = interp[p], interp[p + 4]
        side_out[0, p], side_out[1, p] = pack_pair(near, far)
        for b in range(2):
            side_out[b, 4, pl.ds(p, 1), :] = near[4 - b : 5 - b]
            side_out[b, 4, pl.ds(p + 4, 1), :] = far[4 - b : 5 - b]
            send_piece(1, 2 * b, side_out.at[b, p], side_in.at[1 - b, p])
        send_piece(0, 1, interp.at[p], dom_in.at[1, p])
        send_piece(2, 1, interp.at[p + 4], dom_in.at[0, p + 1])

        @pl.when(q == 0)
        def _():
            send_piece(0, 1, interp.at[4], dom_in.at[1, 4])

        @pl.when(q % 2 == 1)
        def _():
            j = q // 2
            for a in range(2):
                pieces_of = pack_pair(interp[4 * a + j], interp[4 * a + 2 + j])
                for b in range(2):
                    corner_out[a, b, j] = pieces_of[b]
                    send_piece(2 * a, 2 * b, corner_out.at[a, b, j], corner_in.at[1 - a, 1 - b, j])

        @pl.when(q == 3)
        def _():
            send_piece(2, 1, interp.at[3], dom_in.at[0, 0])
            for b in range(2):
                send_piece(1, 2 * b, side_out.at[b, 4], side_in.at[1 - b, 4])

        return carry

    lax.fori_loop(0, 4, plane_pair, 0)

    receive_all(rig_copies)
    unpack_halos(rigidity, rig_side_in, rig_dom_in, rig_corner_in, rig_wide)
    receive_all(copies)
    unpack_halos(interp, side_in, dom_in, corner_in, wide)

    row = lax.broadcasted_iota(jnp.int32, (16, 512), 0)
    lane = lax.broadcasted_iota(jnp.int32, (16, 512), 1)
    row_inside = ((row >= 4) | (s > 0)) & ((row < 12) | (s < slabs - 1))

    def inside(xx):
        return row_inside & ((xx >= 4) | (d > 0)) & ((xx < 12) | (d < doms - 1))

    def back_z(v):
        return jnp.where(lane == 0, 0.0, pltpu.roll(v, 1, 1))

    def ahead_z(v):
        return jnp.where(lane == 511, 0.0, pltpu.roll(v, 511, 1))

    basis = (basis_0, basis_1, basis_2, basis_3)

    def in_groups(first, end, size, body, carry):
        def group(i, carry):
            for k in range(size):
                carry = body(first + size * i + k, carry)
            return carry

        return lax.fori_loop(0, (end - first) // size, group, carry)

    def load_plane(xx, carry):
        here = wide[xx + 1]
        keep = inside(xx)
        at = jnp.clip(xx - 4, 0, 7)
        back = jnp.where(row == 0, side_in[0, 4, pl.ds(at, 1), :], pltpu.roll(here, 1, 0))
        ahead = jnp.where(row == 15, side_in[1, 4, pl.ds(at, 1), :], pltpu.roll(here, 15, 0))
        basis_0[0, xx] = jnp.where(keep, COEF * (wide[xx + 2] - wide[xx]), 0.0)
        basis_0[1, xx] = jnp.where(keep, COEF * (ahead - back), 0.0)
        basis_0[2, xx] = jnp.where(keep, COEF * (ahead_z(here) - back_z(here)), 0.0)
        return carry

    in_groups(0, 16, 4, load_plane, 0)

    def scaled_operate(level, c, xx):
        v = basis[level][c, xx]
        beside = basis[level][c, xx - 1] + basis[level][c, xx + 1]
        beside = beside + pltpu.roll(v, 1, 0) + pltpu.roll(v, 15, 0)
        beside = beside + back_z(v) + ahead_z(v)
        return ((rig_wide[xx + 1] + (6.0 - CENTRE)) * v - beside) * (1.0 / SPREAD)

    for level in range(1, 4):

        def next_plane(xx, carry, level=level):
            keep = inside(xx)
            for c in range(3):
                image = scaled_operate(level - 1, c, xx)
                if level > 1:
                    image = 2.0 * image - basis[level - 2][c, xx]
                basis[level][c, xx] = jnp.where(keep, image, 0.0)
            return carry

        in_groups(level, 16 - level, (7, 4, 5)[level - 1], next_plane, 0)

    def folded(field):
        return jnp.where(low_half(field[:8]), field[8:], field[:8])

    def moment_plane(xx, totals):
        totals = list(totals)
        for c in range(3):
            w = [folded(basis[level][c, xx]) for level in range(4)]
            for level in range(4):
                centre[level, c, xx - 4] = w[level]
            w.append(folded(scaled_operate(3, c, xx)))
            pairs = ((0, 0), (0, 1), (1, 1), (1, 2), (2, 2), (2, 3), (3, 3), (3, 4))
            for i, (one, two) in enumerate(pairs):
                product = w[one] * w[two]
                product = (product[:, :128] + product[:, 128:256]) + (product[:, 256:384] + product[:, 384:])
                totals[i] = totals[i] + product
        return tuple(totals)

    totals = in_groups(4, 12, 4, moment_plane, tuple(jnp.zeros((8, 128), F32) for _ in range(8)))
    for i in range(8):
        dom_moments[0, i : i + 1] = jnp.sum(totals[i], axis=0, keepdims=True)

    def reduce_copy(buffer, send, recv, source, target, device):
        return pltpu.make_async_remote_copy(
            src_ref=buffer.at[source],
            dst_ref=buffer.at[target],
            send_sem=send,
            recv_sem=recv,
            device_id=device,
            device_id_type=MESH,
        )

    for k in range(1, doms):
        reduce_copy(dom_moments, dom_send, dom_recv, 0, k, (lax.rem(d + k, doms), s)).start()
    others = pl.ds(1, doms - 1)
    dom_all = reduce_copy(dom_moments, dom_send, dom_recv, others, others, (lax.rem(d + 1, doms), s))
    others = pl.ds(1, slabs - 1)
    slab_all = reduce_copy(slab_moments, slab_send, slab_recv, others, others, (d, lax.rem(s + 1, slabs)))

    for level in range(4):
        for c in range(3):
            for x in range(8):
                for half in range(2):
                    high, low = two_pieces(centre[level, c, x, :, 256 * half : 256 * half + 256])
                    at = 16 * x + 8 * half
                    at = at + 256 * (3 * level + c)
                    wet_pieces[at : at + 8] = high
                    wet_pieces[128 + at : 136 + at] = low

    def wet_block(a):
        node = jnp.concatenate([wet_position[3 * a + b] for b in range(3)], axis=1)
        group = (node >> 12) * 16 + ((node >> 8) & 1) * 8 + (((node >> 9) + 4) & 7)
        slot = lax.broadcasted_iota(jnp.int32, (1, 128), 1)
        live = jnp.concatenate(
            [slot < wet_tally[0:1, 3 * a + b : 3 * a + b + 1] for b in range(3)], axis=1
        )
        picked = jnp.dot(wet_pieces[...], one_hot(node & 255), preferred_element_type=F32)
        for kc in range(12):
            found = pick_group(picked[256 * kc : 256 * kc + 256], 128, group)
            found = jnp.where(live, jnp.sum(found, axis=0, keepdims=True), 0.0)
            at = kc // 3 * 4 + kc % 3
            for b in range(3):
                wet_out[3 * a + b, at : at + 1] = found[:, 128 * b : 128 * b + 128]

    wet_copies = []
    for j in range(9):
        if j == 4:
            continue
        copy = pltpu.make_async_remote_copy(
            src_ref=wet_out.at[j],
            dst_ref=wet_in.at[8 - j],
            send_sem=wet_send.at[j],
            recv_sem=wet_recv.at[8 - j],
            device_id=(d + (j // 3 - 1), s + (j % 3 - 1)),
            device_id_type=MESH,
        )
        wet_copies.append((j // 3, j % 3, copy))

    def wet_row(a):
        wet_block(a)
        start_all([one for one in wet_copies if one[0] == a])

    wet_row(0)
    dom_all.wait_recv()
    total = dom_moments[0]
    for k in range(1, doms):
        total = total + dom_moments[k]
    slab_moments[0] = total
    for k in range(1, slabs):
        reduce_copy(slab_moments, slab_send, slab_recv, 0, k, (d, lax.rem(s + k, slabs))).start()
    wet_row(2)
    wet_row(1)
    wet_in[4] = wet_out[4]

    taker = jnp.concatenate([accepting[j] for j in range(9)], axis=1)
    lane_of = lax.broadcasted_iota(jnp.int32, (128, 1152), 0)
    lane_hot = jnp.where(lane_of == (taker & 127), 1.0, 0.0).astype(BF16)

    slab_all.wait_recv()
    total = slab_moments[0]
    for k in range(1, slabs):
        total = total + slab_moments[k]
    c = coefficients([jnp.sum(total[i : i + 1], axis=1, keepdims=True) for i in range(8)])

    def combine(x, carry):
        for a in range(3):
            field = c[0] * centre[0, a, x]
            for level in range(1, 4):
                field = field + c[level] * centre[level, a, x]
            disp[a, x] = half_turn(field)
        return carry

    lax.fori_loop(0, 8, combine, 0)

    receive_all(wet_copies)
    sub = lax.broadcasted_iota(jnp.int32, (8, 1), 0)
    first = jnp.where(sub < 4, c[0], c[1])
    second = jnp.where(sub < 4, c[2], c[3])
    value = jnp.concatenate([wet_in[j, :8] * first + wet_in[j, 8:] * second for j in range(9)], axis=1)
    value = value + half_turn(value)
    high = value.astype(BF16).astype(F32)
    apart = (taker >> 7) - (lax.broadcasted_iota(jnp.int32, (8, 1152), 0) >> 2)
    for part_of in range(4):
        at = range(16 * part_of, 16 * part_of + 16)
        lines = [
            jnp.where(apart == 2 * h, part, 0.0).astype(BF16) for part in (high, value - high) for h in at
        ]
        put = lax.dot_general(
            jnp.concatenate(lines, axis=0), lane_hot, (((1,), (1,)), ((), ())), preferred_element_type=F32
        )
        put = put[:128] + put[128:]
        for h in range(32):
            spread[:, 4096 * part_of + 128 * h : 4096 * part_of + 128 * h + 128] = put[4 * h : 4 * h + 3]

    finish_all(rig_copies)
    for j in range(9):
        if j == 4:
            continue

        @pl.when(exists(j // 3, j % 3))
        def _():
            slot_copy(j).wait_send()

    finish_all(copies)
    finish_all(wet_copies)
    dom_all.wait_send()
    slab_all.wait_send()


def on_device(doms, slabs, heat, emitting, shift, bucket, factor, rigidity, position, tally, accepting):
    dma = pltpu.SemaphoreType.DMA
    vm = pltpu.VMEM
    halos_out = [vm((2, 5, 8, 512), F32), vm((2, 2, 2, 8, 512), F32)]
    halos_in = [vm((2, 5, 8, 512), F32), vm((2, 5, 8, 512), F32), vm((2, 2, 2, 8, 512), F32)]
    halos = [halos_out[0], halos_in[0], halos_in[1], halos_out[1], halos_in[2]]
    whole = pl.BlockSpec(memory_space=pltpu.VMEM)
    away = pl.BlockSpec(memory_space=pl.ANY)
    return pl.pallas_call(
        functools.partial(kernel, doms, slabs),
        out_shape=[
            jax.ShapeDtypeStruct((3, 8, 8, 512), F32),
            jax.ShapeDtypeStruct((3, 16384), F32),
        ],
        in_specs=[whole, whole, away, away, away, whole, whole, whole, whole],
        out_specs=[whole, whole],
        scratch_shapes=[
            vm((4, 8, 8, 512), jnp.int32),
            vm((4, 8, 8, 512), jnp.int32),
            vm((4, 8, 8, 512), F32),
            vm((128, 256), BF16),
            vm((9, 64, 128), F32),
            vm((9, 64, 128), F32),
            vm((576, 256), BF16),
            vm((8, 8, 512), F32),
            *halos,
            *halos,
            vm((18, 16, 512), F32),
            vm((18, 16, 512), F32),
            *[vm((3, 16, 16, 512), F32) for _ in range(4)],
            vm((4, 3, 8, 8, 512), F32),
            vm((doms, 8, 128), F32),
            vm((slabs, 8, 128), F32),
            vm((3072, 256), BF16),
            vm((9, 16, 128), F32),
            vm((9, 16, 128), F32),
            dma((3,)),
            dma((9,)),
            dma((9,)),
            dma((9,)),
            dma((9,)),
            dma((9,)),
            dma((9,)),
            dma((9,)),
            dma((9,)),
            dma,
            dma,
            dma,
            dma,
        ],
        compiler_params=pltpu.CompilerParams(
            collective_id=0, has_side_effects=True, vmem_limit_bytes=56 * 2**20
        ),
    )(
        heat.reshape(128, 128),
        emitting.reshape(576, 128),
        shift,
        bucket,
        factor,
        rigidity,
        position.reshape(9, 1, 128),
        tally,
        accepting.reshape(9, 1, 128),
    )


def solution(mesh):
    in_specs = (
        P(BOTH),
        P(BOTH, None, None, None),
        P(None, DOM, SLAB, None),
        P(None, DOM, SLAB, None),
        P(None, DOM, SLAB, None),
        P(DOM, SLAB, None),
        P(BOTH, None, None, None),
        P(BOTH, None),
        P(BOTH, None, None, None),
    )
    out_specs = (P(None, DOM, SLAB, None), P(None, BOTH))
    return jax.shard_map(
        functools.partial(on_device, mesh.shape[DOM], mesh.shape[SLAB]),
        mesh=mesh,
        in_specs=in_specs,
        out_specs=out_specs,
        check_vma=False,
    )
```
